32 devices in a mesh: groups: 2 (over y), samp: 4 (over z), head: 4 (over x, core).
Axes of the slice: x: 2, y: 2, z: 4, core: 2. Of those that a mesh axis runs over, the one named last changes fastest.
Arguments:
- prompt_states: bfloat16 [8, 1024, 5120], P(('groups', 'samp'), None, 'head'), parts along dimension 0, may hold values from -6 to 6
- prompt_lengths: int32 [8], P('groups'), parts along dimension 0, may hold values from 1 to 1024, 2048 in all
- prompt_owner: int32 [8], P('groups'), parts along dimension 0, may hold values from 0 to 3, each once
- kv_weight: bfloat16 [5120, 2048], P('head'), may hold values from -0.078125 to 0.078125
- sampler_prompts: int32 [16], P(('groups', 'samp')), parts along dimension 0, may hold values from 0 to 3, as said below
- step_queries: bfloat16 [4, 512, 5120], P(None, ('groups', 'samp'), 'head'), parts along dimension 1, may hold values from -8 to 8
- step_kv: bfloat16 [4, 512, 2048], P(None, ('groups', 'samp'), 'head'), parts along dimension 1, may hold values from -8 to 8
- out_weight: bfloat16 [5120, 5120], P('head', 'samp'), may hold values from -0.625 to 0.625
Outputs:
- mixed: bfloat16 [4, 512, 5120], P(None, ('groups', 'samp'), 'head'), parts along dimension 1
The draws below stay inside these ranges and needn't reach their ends.
There are 2 independent parts, one for each index of `groups`. The reference program is written for one: setup_inputs(seed, part) draws one part's arguments, and reference() takes and returns one part's arrays. A program takes and returns all parts, laid end to end along the dimension named above; an argument that names none is the same for every part. Nothing has to cross between parts.
Inputs may be any that keep to these rules, and one draw needn't show every extreme that they name: prompt_owner is a permutation: each owner slot holds exactly one prompt. `sampler_prompts`: entries s * 2 to s * 2 + 1 are 2 different prompts, one for each of sampler s's aligned blocks of 32 rows in order; every prompt is listed by at least one sampler.
All inputs are finite; a program needn't handle non-finite values.
Results may differ from the reference program's by a relative error of at most 0.017.
Values may be sent and summed in bfloat16 or wider, within the bound.
No kernel may reach another device: no remote copies, remote signals or barrier semaphores. Data moves between devices by JAX's collectives and lax.ppermute only.
A program may use at most 128 MiB of HBM per device.

```python
import math
import jax
import jax.numpy as jnp
import numpy as np
from jax import lax

D = 5120
NH = 40
KVH = 8
HD = 128
GQA = 5
LMAX = 1024
BLK = 32
STEPS = 4
MAXP = 2
PROMPTS = 4
ROWS = 256
N_HEAD = 4


def draw_step_queries(key, part):
    key = jax.random.fold_in(key, 5)
    values = 1.5 * jax.random.truncated_normal(key, -4.0, 4.0, (STEPS, ROWS, KVH, GQA, HD), jnp.float32)
    return values.reshape(STEPS, ROWS, NH * HD).astype(jnp.bfloat16)


def draw_step_kv(key, part):
    key = jax.random.fold_in(key, 7)
    values = 2.0 * jax.random.truncated_normal(key, -4.0, 4.0, (STEPS, ROWS, KVH, 2, HD), jnp.float32)
    return values.reshape(STEPS, ROWS, 2 * KVH * HD).astype(jnp.bfloat16)


def draw_sampler_prompts(key, part):
    key = jax.random.fold_in(key, 11)
    first_key, popular_key, jitter_key = jax.random.split(key, 3)
    leading = jax.random.permutation(first_key, PROMPTS).astype(jnp.int32)
    popularity = jax.random.randint(popular_key, (1, PROMPTS), 0, 2048)
    jitter = jax.random.randint(jitter_key, (PROMPTS, PROMPTS), 0, 1024)
    columns = jnp.arange(PROMPTS, dtype=jnp.int32)[None, :]
    scores = (jitter + popularity) * PROMPTS + columns
    scores = jnp.where(columns == leading[:, None], -1, scores)
    others = lax.top_k(scores, MAXP - 1)[1]
    listing = jnp.concatenate([leading[:, None], others.astype(jnp.int32)], axis=1)
    return listing.reshape(PROMPTS * MAXP).astype(jnp.int32)


def shard_levels(own_key, dims, pieces, least, largest):
    loudness = 1.0
    for axis_at, parts in pieces:
        draws = jax.random.uniform(jax.random.fold_in(jax.random.fold_in(own_key, 6), axis_at), (parts,), jnp.float32, least / len(pieces), largest / len(pieces))
        loudness = loudness * jnp.repeat(jnp.exp(draws), dims[axis_at] // parts).reshape((-1,) + (1,) * (len(dims) - 1 - axis_at))
    return loudness


def split_up(count, total, limit, lean):
    portions = [(1 << 20) // math.isqrt(grade ** lean) + 1 for grade in range(2, count + 1)]
    spare, holding = total - limit - (count - 1), [1] * (count - 1)
    while spare > 0:
        movable = [i for i in range(count - 1) if holding[i] < limit]
        pool, budget = sum([portions[i] for i in movable]), spare
        for i in movable:
            extra = min(limit - holding[i], max(1, budget * portions[i] // pool), spare)
            holding[i] = holding[i] + extra
            spare = spare - extra
    return np.array([limit] + holding)


def uneven_parts(own_key, count, total, most, lean):
    if count == 2:
        one = jax.random.randint(own_key, (), max(1, total - most), min(most, total - 1) + 1)
        return jnp.stack([one, total - one])
    tallies = jnp.asarray(split_up(count, total, most, lean), jnp.int32)
    couples = (count - 1) // 2
    giver, receiver = tallies[1:1 + 2 * couples:2], tallies[2:2 + 2 * couples:2]
    slack = jnp.minimum(giver - 1, most - receiver)
    moved = jax.random.randint(jax.random.fold_in(own_key, 1), (couples,), 0, 1 << 20) % (slack + 1)
    tallies = tallies.at[1:1 + 2 * couples:2].set(giver - moved).at[2:2 + 2 * couples:2].set(receiver + moved)
    return tallies[jax.random.permutation(jax.random.fold_in(own_key, 2), count)]


def centred(rng, extent, spread, most, pieces=(), kind=jnp.bfloat16):
    entries = jax.random.normal(rng, extent, jnp.float32) * spread
    if len(pieces) > 0:
        entries = shard_levels(rng, extent, pieces, -0.22, 0.18) * entries
    return jnp.clip(entries, min=-most, max=most).astype(kind)


def setup_inputs(seed: int = 0, part: int = 0) -> dict:
    keys = jax.random.split(jax.random.key(seed), 9)
    own_keys = jax.random.split(jax.random.fold_in(keys[8], part), 9)
    return {
        "prompt_states": centred(own_keys[0], (PROMPTS, LMAX, D), 1.0, 6.0, ((0, 4), (2, 4))),
        "prompt_lengths": uneven_parts(own_keys[1], PROMPTS, PROMPTS * LMAX // 2, LMAX, 1).astype(jnp.int32),
        "prompt_owner": jax.random.permutation(own_keys[2], PROMPTS).astype(jnp.int32),
        "kv_weight": centred(keys[3], (D, 2 * KVH * HD), D ** -0.5, 0.078125, ((0, 4),)),
        "sampler_prompts": draw_sampler_prompts(jax.random.fold_in(jax.random.fold_in(keys[8], part), 71), part),
        "step_queries": draw_step_queries(jax.random.fold_in(jax.random.fold_in(keys[8], part), 71), part),
        "step_kv": draw_step_kv(jax.random.fold_in(jax.random.fold_in(keys[8], part), 71), part),
        "out_weight": centred(keys[7], (NH * HD, D), (NH * HD // 64) ** -0.5, 0.625, ((0, 4), (1, 4))),
    }


masked_score = -1e+30

def prefill_pages(prompt_states, kv_weight):
    feature_block = D // N_HEAD
    weight_blocks = kv_weight.reshape(N_HEAD, feature_block, 2 * KVH * HD).astype(jnp.float32)

    def one_prompt(states):
        split_states = states.reshape(LMAX, N_HEAD, feature_block).astype(jnp.float32)
        partials = jnp.einsum('lhf,hfc->hlc', split_states, weight_blocks).astype(jnp.bfloat16)
        partials = lax.optimization_barrier(partials).astype(jnp.float32)
        return lax.optimization_barrier(jnp.sum(partials, axis=0)).astype(jnp.bfloat16)
    return lax.map(one_prompt, prompt_states)

def reference(prompt_states, prompt_lengths, prompt_owner, kv_weight, sampler_prompts, step_queries, step_kv, out_weight):
    pages = prefill_pages(prompt_states, kv_weight).reshape(PROMPTS, LMAX, KVH, 2, HD)
    block_count = PROMPTS * MAXP
    queries = step_queries.reshape(STEPS, block_count, BLK, KVH, GQA, HD)
    own_cache = step_kv.reshape(STEPS, block_count, BLK, KVH, 2, HD)
    score_scale = 1.0 / math.sqrt(HD)
    key_places = jnp.arange(LMAX, dtype=jnp.int32)
    causal = jnp.arange(STEPS, dtype=jnp.int32)[None, :] <= jnp.arange(STEPS, dtype=jnp.int32)[:, None]

    def block_attention(index):
        prompt = sampler_prompts[index]
        owner_slot = prompt_owner[prompt]
        length = prompt_lengths[prompt]
        page_block = lax.dynamic_index_in_dim(pages, owner_slot, 0, keepdims=False).astype(jnp.float32)
        query_block = lax.dynamic_index_in_dim(queries, index, 1, keepdims=False).astype(jnp.float32)
        own_block = lax.dynamic_index_in_dim(own_cache, index, 1, keepdims=False).astype(jnp.float32)
        far_scores = jnp.einsum('tbgjd,lgd->tbgjl', query_block, page_block[:, :, 0]) * score_scale
        near_scores = jnp.einsum('tbgjd,ubgd->tbgju', query_block, own_block[:, :, :, 0]) * score_scale
        far_usable = (key_places < length)[None, None, None, None, :]
        near_usable = causal[:, None, None, None, :]
        peak_score = jnp.maximum(lax.optimization_barrier(jnp.max(jnp.where(far_usable, far_scores, masked_score), axis=4)), lax.optimization_barrier(jnp.max(jnp.where(near_usable, near_scores, masked_score), axis=4)))
        far_weights = jnp.where(far_usable, jnp.exp(far_scores - peak_score[..., None]), 0.0)
        near_weights = jnp.where(near_usable, jnp.exp(near_scores - peak_score[..., None]), 0.0)
        totals = lax.optimization_barrier(jnp.sum(far_weights, axis=4)) + lax.optimization_barrier(jnp.sum(near_weights, axis=4))
        far_rounded = lax.optimization_barrier(far_weights.astype(jnp.bfloat16)).astype(jnp.float32)
        near_rounded = lax.optimization_barrier(near_weights.astype(jnp.bfloat16)).astype(jnp.float32)
        summed = jnp.einsum('tbgjl,lgd->tbgjd', far_rounded, page_block[:, :, 1])
        summed = summed + jnp.einsum('tbgju,ubgd->tbgjd', near_rounded, own_block[:, :, :, 1])
        return (summed / totals[..., None]).astype(jnp.bfloat16)
    attention = lax.map(block_attention, jnp.arange(block_count, dtype=jnp.int32))
    attention = jnp.moveaxis(attention, 0, 1).reshape(STEPS * ROWS, NH * HD)
    head_block = NH * HD // N_HEAD
    split_attention = attention.reshape(STEPS * ROWS, N_HEAD, head_block)
    split_weight = out_weight.reshape(N_HEAD, head_block, D)
    mixed = jnp.zeros((STEPS * ROWS, D), jnp.float32)
    for shard_index in range(N_HEAD):
        partial_value = jnp.dot(split_attention[:, shard_index], split_weight[shard_index], preferred_element_type=jnp.float32)
        partial_value = lax.optimization_barrier(partial_value.astype(jnp.bfloat16)).astype(jnp.float32)
        mixed = mixed + partial_value
    return mixed.astype(jnp.bfloat16).reshape(STEPS, ROWS, D)
```

```python
import math

import jax
import jax.numpy as jnp
from jax import lax
from jax.experimental import pallas as pl
from jax.experimental.pallas import tpu as pltpu
from jax.sharding import PartitionSpec as P

HD = 128
GQA = 5


masked_score = -1e30


def prompt_partial(queries, page_block, length):
    row_count = queries.shape[0]
    groups = page_block.shape[0] // (2 * HD)
    score_scale = 1.0 / math.sqrt(HD)
    query_heads = queries.reshape(row_count, groups, GQA, HD)
    page_heads = page_block.reshape(groups, 2, HD, page_block.shape[1])
    scores = (
        jnp.einsum(
            "rgjd,gdl->grjl", query_heads, page_heads[:, 0], preferred_element_type=jnp.float32
        )
        * score_scale
    )
    usable = lax.broadcasted_iota(jnp.int32, scores.shape, 3) < length
    peak_score = jnp.max(jnp.where(usable, scores, masked_score), axis=3)
    weights = jnp.where(usable, jnp.exp(scores - peak_score[..., None]), 0.0)
    totals = jnp.sum(weights, axis=3)
    summed = jnp.einsum(
        "grjl,gdl->grjd",
        weights.astype(jnp.bfloat16),
        page_heads[:, 1],
        preferred_element_type=jnp.float32,
    )
    summed = jnp.transpose(summed, (1, 0, 2, 3)).reshape(row_count, groups * GQA * HD)
    peak_score = jnp.transpose(peak_score, (1, 0, 2)).reshape(row_count, groups * GQA)
    totals = jnp.transpose(totals, (1, 0, 2)).reshape(row_count, groups * GQA)
    return (summed, peak_score, totals)


def general_plan(
    prompt_states,
    prompt_lengths,
    prompt_owner,
    kv_weight,
    sampler_prompts,
    step_queries,
    step_kv,
    out_weight,
):
    states = prompt_states[0]
    own_pages = lax.psum_scatter(
        lax.dot_general(
            kv_weight, states, (((0,), (1,)), ((), ())), preferred_element_type=jnp.float32
        ).astype(jnp.bfloat16),
        "head",
        scatter_dimension=0,
        tiled=True,
    )
    step_count = step_queries.shape[0]
    row_total = step_queries.shape[1]
    prompt_count = sampler_prompts.shape[0]
    block_rows = row_total // prompt_count
    head_width = step_queries.shape[2]
    groups = own_pages.shape[0] // (2 * HD)
    owner_slots = jnp.take(prompt_owner, sampler_prompts)
    block_lengths = jnp.take(prompt_lengths, sampler_prompts)
    block_queries = [
        step_queries[:, position * block_rows : (position + 1) * block_rows].reshape(
            step_count * block_rows, head_width
        )
        for position in range(prompt_count)
    ]
    library = lax.all_gather(own_pages[None], "samp", axis=0, tiled=True)
    partials = []
    for position in range(prompt_count):
        page_block = lax.dynamic_index_in_dim(library, owner_slots[position], 0, keepdims=False)
        partials.append(
            prompt_partial(block_queries[position], page_block, block_lengths[position])
        )
    prompt_sum = jnp.concatenate(
        [entry[0].reshape(step_count, block_rows, groups, GQA, HD) for entry in partials], axis=1
    )
    prompt_peak = jnp.concatenate(
        [entry[1].reshape(step_count, block_rows, groups, GQA) for entry in partials], axis=1
    )
    prompt_total = jnp.concatenate(
        [entry[2].reshape(step_count, block_rows, groups, GQA) for entry in partials], axis=1
    )
    score_scale = 1.0 / math.sqrt(HD)
    query_all = step_queries.reshape(step_count, row_total, groups, GQA, HD)
    own_cache = step_kv.reshape(step_count, row_total, groups, 2, HD)
    near_scores = (
        jnp.einsum(
            "trgjd,urgd->trgju",
            query_all,
            own_cache[:, :, :, 0],
            preferred_element_type=jnp.float32,
        )
        * score_scale
    )
    causal = lax.broadcasted_iota(jnp.int32, near_scores.shape, 4) <= lax.broadcasted_iota(
        jnp.int32, near_scores.shape, 0
    )
    near_peak = jnp.max(jnp.where(causal, near_scores, masked_score), axis=4)
    near_weights = jnp.where(causal, jnp.exp(near_scores - near_peak[..., None]), 0.0)
    near_total = jnp.sum(near_weights, axis=4)
    near_sum = jnp.einsum(
        "trgju,urgd->trgjd",
        near_weights.astype(jnp.bfloat16),
        own_cache[:, :, :, 1],
        preferred_element_type=jnp.float32,
    )
    peak_all = jnp.maximum(prompt_peak, near_peak)
    far_factor = jnp.exp(prompt_peak - peak_all)
    near_factor = jnp.exp(near_peak - peak_all)
    numerator = prompt_sum * far_factor[..., None] + near_sum * near_factor[..., None]
    denominator = prompt_total * far_factor + near_total * near_factor
    attention = (numerator / denominator[..., None]).astype(jnp.bfloat16)
    attention = attention.reshape(step_count * row_total, groups * GQA * HD)
    terms = jnp.dot(
        attention,
        lax.all_gather(out_weight, "samp", axis=1, tiled=True),
        preferred_element_type=jnp.float32,
    )
    mixed = lax.psum_scatter(
        terms.astype(jnp.bfloat16), "head", scatter_dimension=1, tiled=True
    ).astype(jnp.float32)
    return mixed.astype(jnp.bfloat16).reshape(step_count, row_total, mixed.shape[1])


CHUNKS = 4
PIECES = 2
VMEM = 56 * 1024 * 1024

CORE = [(0, 1), (1, 0), (2, 3), (3, 2)]
ACROSS_X = [(0, 2), (2, 0), (1, 3), (3, 1)]
INWARD = [(0, 1), (3, 2)]
OUTWARD = [(1, 0), (2, 3)]
MIDDLE = [(1, 2), (2, 1)]
BEYOND = [(1, 3), (2, 0)]


def compiler_params():
    return pltpu.CompilerParams(vmem_limit_bytes=VMEM)


def project(states, weight, first, second):
    tokens, features = states.shape
    width = weight.shape[1] // 4
    chunk = tokens // CHUNKS

    def body(places, state_ref, first_ref, second_ref, *outs):
        step = pl.program_id(0)
        one = jnp.dot(state_ref[...], first_ref[...], preferred_element_type=jnp.float32)
        two = jnp.dot(state_ref[...], second_ref[...], preferred_element_type=jnp.float32)
        for at in range(CHUNKS):

            @pl.when(step == at)
            def _():
                outs[at][...] = one.astype(jnp.bfloat16)
                outs[CHUNKS + at][...] = two.astype(jnp.bfloat16)

    whole = pl.BlockSpec((chunk, width), lambda i, places: (0, 0))
    outs = pl.pallas_call(
        body,
        grid_spec=pltpu.PrefetchScalarGridSpec(
            num_scalar_prefetch=1,
            grid=(CHUNKS,),
            in_specs=[
                pl.BlockSpec((chunk, features), lambda i, places: (i, 0)),
                pl.BlockSpec((features, width), lambda i, places: (0, places[0])),
                pl.BlockSpec((features, width), lambda i, places: (0, places[1])),
            ],
            out_specs=[whole] * (2 * CHUNKS),
        ),
        out_shape=[jax.ShapeDtypeStruct((chunk, width), jnp.bfloat16)] * (2 * CHUNKS),
        compiler_params=compiler_params(),
        name="project",
    )(jnp.stack([first, second]).astype(jnp.int32), states, weight, weight)
    return outs[:CHUNKS], outs[CHUNKS:]


def attend(places, lengths, queries, news, pages):
    steps, rows, width = queries.shape
    blocks = places.shape[0]
    block_rows = rows // blocks
    new_width = news.shape[2]
    groups = new_width // (2 * HD)
    chunk = pages[0][0].shape[0]
    tokens = chunk * CHUNKS
    flat = steps * block_rows
    factor = math.log2(math.e) / math.sqrt(HD)

    def body(places_ref, lengths_ref, query_ref, new_ref, *rest):
        page_refs, out_ref, held = rest[: 4 * CHUNKS], rest[4 * CHUNKS], rest[4 * CHUNKS + 1]
        block = pl.program_id(0)
        place, length = places_ref[block], lengths_ref[block]
        for which in range(4):

            @pl.when(place == which)
            def _():
                for at in range(CHUNKS):
                    held[at * chunk : (at + 1) * chunk] = page_refs[which * CHUNKS + at][...]

        query = query_ref[...].reshape(flat, width)
        new = new_ref[...].reshape(flat, new_width)
        shape = (GQA * flat, flat)
        asker = lax.broadcasted_iota(jnp.int32, shape, 0) % flat
        holder = lax.broadcasted_iota(jnp.int32, shape, 1)
        same_row = asker % block_rows == holder % block_rows
        near_ok = jnp.logical_and(same_row, holder <= asker)
        far_ok = lax.broadcasted_iota(jnp.int32, (GQA * flat, tokens), 1) < length
        for group in range(groups):
            key = slice(2 * group * HD, (2 * group + 1) * HD)
            value = slice((2 * group + 1) * HD, (2 * group + 2) * HD)
            asked = jnp.concatenate(
                [
                    query[:, (group * GQA + head) * HD : (group * GQA + head + 1) * HD]
                    for head in range(GQA)
                ],
                axis=0,
            )
            far = lax.dot_general(
                asked, held[:, key], (((1,), (1,)), ((), ())), preferred_element_type=jnp.float32
            )
            near = lax.dot_general(
                asked, new[:, key], (((1,), (1,)), ((), ())), preferred_element_type=jnp.float32
            )
            far = jnp.where(far_ok, far * factor, masked_score)
            near = jnp.where(near_ok, near * factor, masked_score)
            peak = jnp.maximum(
                jnp.max(far, axis=1, keepdims=True), jnp.max(near, axis=1, keepdims=True)
            )
            far = jnp.exp2(far - peak)
            near = jnp.exp2(near - peak)
            total = jnp.sum(far, axis=1, keepdims=True) + jnp.sum(near, axis=1, keepdims=True)
            summed = jnp.dot(
                far.astype(jnp.bfloat16), held[:, value], preferred_element_type=jnp.float32
            ) + jnp.dot(near.astype(jnp.bfloat16), new[:, value], preferred_element_type=jnp.float32)
            result = (summed / total).astype(jnp.bfloat16)
            for head in range(GQA):
                column = (group * GQA + head) * HD
                out_ref[:, :, column : column + HD] = result[
                    head * flat : (head + 1) * flat
                ].reshape(steps, block_rows, HD)

    page_spec = pl.BlockSpec((chunk, new_width), lambda i, p, n: (0, 0))
    return pl.pallas_call(
        body,
        grid_spec=pltpu.PrefetchScalarGridSpec(
            num_scalar_prefetch=2,
            grid=(blocks,),
            in_specs=[
                pl.BlockSpec((steps, block_rows, width), lambda i, p, n: (0, i, 0)),
                pl.BlockSpec((steps, block_rows, new_width), lambda i, p, n: (0, i, 0)),
            ]
            + [page_spec] * (4 * CHUNKS),
            out_specs=pl.BlockSpec((steps, block_rows, width), lambda i, p, n: (0, i, 0)),
            scratch_shapes=[pltpu.VMEM((tokens, new_width), jnp.bfloat16)],
        ),
        out_shape=jax.ShapeDtypeStruct(queries.shape, jnp.bfloat16),
        compiler_params=compiler_params(),
        name="attend",
    )(places, lengths, queries, news, *[part for page in pages for part in page])


def spread(flag, attention, own_weight, moved_weight):
    steps, rows, features = attention.shape
    columns = own_weight.shape[1]
    tile = 256 if columns % 256 == 0 else columns
    flat = attention.reshape(steps * rows, features)

    def body(flag_ref, rows_ref, own_ref, moved_ref, keep_ref, send_ref):
        own = jnp.dot(rows_ref[...], own_ref[...], preferred_element_type=jnp.float32)
        moved = jnp.dot(rows_ref[...], moved_ref[...], preferred_element_type=jnp.float32)
        keeps_own = flag_ref[0] == 1
        keep_ref[...] = jnp.where(keeps_own, own, moved).astype(jnp.bfloat16)
        send_ref[...] = jnp.where(keeps_own, moved, own).astype(jnp.bfloat16)

    column_spec = pl.BlockSpec((features, tile), lambda i, f: (0, i))
    out_spec = pl.BlockSpec((steps * rows, tile), lambda i, f: (0, i))
    out_shape = jax.ShapeDtypeStruct((steps * rows, columns), jnp.bfloat16)
    keep, send = pl.pallas_call(
        body,
        grid_spec=pltpu.PrefetchScalarGridSpec(
            num_scalar_prefetch=1,
            grid=(columns // tile,),
            in_specs=[
                pl.BlockSpec((steps * rows, features), lambda i, f: (0, 0)),
                column_spec,
                column_spec,
            ],
            out_specs=[out_spec, out_spec],
        ),
        out_shape=[out_shape, out_shape],
        compiler_params=compiler_params(),
        name="spread",
    )(flag, flat, own_weight, moved_weight)
    return keep.reshape(steps, rows, columns), send.reshape(steps, rows, columns)


def added(*parts):
    total = parts[0].astype(jnp.float32)
    for part in parts[1:]:
        total = total + part.astype(jnp.float32)
    return total.astype(jnp.bfloat16)


def inward_plan(
    prompt_states,
    prompt_lengths,
    prompt_owner,
    kv_weight,
    sampler_prompts,
    step_queries,
    step_kv,
    out_weight,
):
    group, plane, head = (lax.axis_index(name) for name in ("groups", "samp", "head"))
    chip, core = head // 2, head % 2
    steps = step_queries.shape[0]

    def on_samp(value, pairs):
        return lax.ppermute(value, "samp", pairs)

    def on_head(value, pairs):
        return lax.ppermute(value, "head", pairs)

    end_prompts = on_samp(sampler_prompts, INWARD)
    end_queries = on_samp(step_queries, INWARD)
    end_news = on_samp(step_kv, INWARD)

    def table(prompts):
        slots = jnp.take(prompt_owner, prompts)
        places = jnp.where(
            slots == plane,
            0,
            jnp.where(slots == (plane ^ 1), 1, jnp.where(slots == 3 - plane, 2, 3)),
        )
        return places.astype(jnp.int32), jnp.take(prompt_lengths, prompts)

    states = prompt_states[0]
    sent, kept = project(states, kv_weight, head ^ 3, head ^ 2)
    crossing = []
    for at in range(CHUNKS):
        crossing.append(on_head(added(kept[at], on_head(sent[at], CORE)), ACROSS_X))
    sent, kept = project(states, kv_weight, head ^ 1, head)
    own_page, end_page, far_page, far_end_page = [], [], [], []
    for at in range(CHUNKS):
        part = added(kept[at], on_head(sent[at], CORE), crossing[at])
        own_page.append(part)
        end_page.append(on_samp(part, INWARD))
        far_page.append(on_samp(part, MIDDLE))
        far_end_page.append(on_samp(end_page[at], MIDDLE))
    pages = (own_page, end_page, far_page, far_end_page)

    half = out_weight.shape[0] // 2
    piece = half // PIECES
    mine, other = [], []
    for at in range(PIECES):
        moving = lax.dynamic_slice_in_dim(out_weight, group * half + at * piece, piece, 0)
        moving, _ = lax.optimization_barrier((moving, own_page[1]))
        mine.append(on_samp(moving, INWARD))
        other.append(lax.ppermute(mine[at], "groups", [(0, 1), (1, 0)]))
    mine, other = jnp.concatenate(mine, axis=0), jnp.concatenate(other, axis=0)
    moved_weight = jnp.where(
        group == 0,
        jnp.concatenate([mine, other], axis=0),
        jnp.concatenate([other, mine], axis=0),
    )

    end_rows = attend(*table(end_prompts), end_queries, end_news, pages)
    far_end_rows = on_samp(end_rows, MIDDLE)
    own_rows = attend(*table(sampler_prompts), step_queries, step_kv, pages)
    far_rows = on_samp(own_rows, MIDDLE)

    flag = (core == plane % 2).astype(jnp.int32).reshape(1)

    def summed(rows):
        keep, send = spread(flag, rows, out_weight, moved_weight)
        arrived = on_head(send, CORE)

        def half_of(value, which):
            return lax.dynamic_slice_in_dim(value, which * (steps // 2), steps // 2, 0)

        leaving = added(half_of(keep, 1 - chip), half_of(arrived, 1 - chip))
        return added(half_of(keep, chip), half_of(arrived, chip), on_head(leaving, ACROSS_X))

    end_sum = summed(end_rows)
    near_out = on_samp(end_sum, OUTWARD)
    own_sum = summed(own_rows)
    beyond_out = on_samp(summed(far_end_rows), BEYOND)
    middle_out = on_samp(summed(far_rows), MIDDLE)

    is_middle = jnp.logical_or(plane == 1, plane == 2)
    near = jnp.where(is_middle, own_sum, near_out)
    far = jnp.where(is_middle, middle_out, beyond_out)
    near_side = chip == plane // 2
    stays = jnp.where(near_side, near, far)
    comes = on_head(jnp.where(near_side, far, near), ACROSS_X)
    return jnp.where(
        chip == 0,
        jnp.concatenate([stays, comes], axis=0),
        jnp.concatenate([comes, stays], axis=0),
    )


def solution(mesh):
    line, width = mesh.shape["samp"], mesh.shape["head"]
    paired = line == 4 and width == 4 and mesh.shape["groups"] == 2
    on_device = inward_plan if paired else general_plan

    placed = (
        P(("groups", "samp"), None, "head"),
        P("groups"),
        P("groups"),
        P("head", None),
        P(("groups", "samp")),
        P(None, ("groups", "samp"), "head"),
        P(None, ("groups", "samp"), "head"),
        P("head", "samp"),
    )
    return jax.shard_map(
        on_device,
        mesh=mesh,
        in_specs=placed,
        out_specs=P(None, ("groups", "samp"), "head"),
        check_vma=False,
    )
```

```python
import math

import jax
import jax.numpy as jnp
from jax import lax
from jax.experimental import pallas as pl
from jax.experimental.pallas import tpu as pltpu
from jax.sharding import PartitionSpec as P

HD = 128
GQA = 5


masked_score = -1e30


def prompt_partial(queries, page_block, length):
    row_count = queries.shape[0]
    groups = page_block.shape[0] // (2 * HD)
    score_scale = 1.0 / math.sqrt(HD)
    query_heads = queries.reshape(row_count, groups, GQA, HD)
    page_heads = page_block.reshape(groups, 2, HD, page_block.shape[1])
    scores = (
        jnp.einsum(
            "rgjd,gdl->grjl", query_heads, page_heads[:, 0], preferred_element_type=jnp.float32
        )
        * score_scale
    )
    usable = lax.broadcasted_iota(jnp.int32, scores.shape, 3) < length
    peak_score = jnp.max(jnp.where(usable, scores, masked_score), axis=3)
    weights = jnp.where(usable, jnp.exp(scores - peak_score[..., None]), 0.0)
    totals = jnp.sum(weights, axis=3)
    summed = jnp.einsum(
        "grjl,gdl->grjd",
        weights.astype(jnp.bfloat16),
        page_heads[:, 1],
        preferred_element_type=jnp.float32,
    )
    summed = jnp.transpose(summed, (1, 0, 2, 3)).reshape(row_count, groups * GQA * HD)
    peak_score = jnp.transpose(peak_score, (1, 0, 2)).reshape(row_count, groups * GQA)
    totals = jnp.transpose(totals, (1, 0, 2)).reshape(row_count, groups * GQA)
    return (summed, peak_score, totals)


def general_plan(
    prompt_states,
    prompt_lengths,
    prompt_owner,
    kv_weight,
    sampler_prompts,
    step_queries,
    step_kv,
    out_weight,
):
    states = prompt_states[0]
    own_pages = lax.psum_scatter(
        lax.dot_general(
            kv_weight, states, (((0,), (1,)), ((), ())), preferred_element_type=jnp.float32
        ).astype(jnp.bfloat16),
        "head",
        scatter_dimension=0,
        tiled=True,
    )
    step_count = step_queries.shape[0]
    row_total = step_queries.shape[1]
    prompt_count = sampler_prompts.shape[0]
    block_rows = row_total // prompt_count
    head_width = step_queries.shape[2]
    groups = own_pages.shape[0] // (2 * HD)
    owner_slots = jnp.take(prompt_owner, sampler_prompts)
    block_lengths = jnp.take(prompt_lengths, sampler_prompts)
    block_queries = [
        step_queries[:, position * block_rows : (position + 1) * block_rows].reshape(
            step_count * block_rows, head_width
        )
        for position in range(prompt_count)
    ]
    library = lax.all_gather(own_pages[None], "samp", axis=0, tiled=True)
    partials = []
    for position in range(prompt_count):
        page_block = lax.dynamic_index_in_dim(library, owner_slots[position], 0, keepdims=False)
        partials.append(
            prompt_partial(block_queries[position], page_block, block_lengths[position])
        )
    prompt_sum = jnp.concatenate(
        [entry[0].reshape(step_count, block_rows, groups, GQA, HD) for entry in partials], axis=1
    )
    prompt_peak = jnp.concatenate(
        [entry[1].reshape(step_count, block_rows, groups, GQA) for entry in partials], axis=1
    )
    prompt_total = jnp.concatenate(
        [entry[2].reshape(step_count, block_rows, groups, GQA) for entry in partials], axis=1
    )
    score_scale = 1.0 / math.sqrt(HD)
    query_all = step_queries.reshape(step_count, row_total, groups, GQA, HD)
    own_cache = step_kv.reshape(step_count, row_total, groups, 2, HD)
    near_scores = (
        jnp.einsum(
            "trgjd,urgd->trgju",
            query_all,
            own_cache[:, :, :, 0],
            preferred_element_type=jnp.float32,
        )
        * score_scale
    )
    causal = lax.broadcasted_iota(jnp.int32, near_scores.shape, 4) <= lax.broadcasted_iota(
        jnp.int32, near_scores.shape, 0
    )
    near_peak = jnp.max(jnp.where(causal, near_scores, masked_score), axis=4)
    near_weights = jnp.where(causal, jnp.exp(near_scores - near_peak[..., None]), 0.0)
    near_total = jnp.sum(near_weights, axis=4)
    near_sum = jnp.einsum(
        "trgju,urgd->trgjd",
        near_weights.astype(jnp.bfloat16),
        own_cache[:, :, :, 1],
        preferred_element_type=jnp.float32,
    )
    peak_all = jnp.maximum(prompt_peak, near_peak)
    far_factor = jnp.exp(prompt_peak - peak_all)
    near_factor = jnp.exp(near_peak - peak_all)
    numerator = prompt_sum * far_factor[..., None] + near_sum * near_factor[..., None]
    denominator = prompt_total * far_factor + near_total * near_factor
    attention = (numerator / denominator[..., None]).astype(jnp.bfloat16)
    attention = attention.reshape(step_count * row_total, groups * GQA * HD)
    terms = jnp.dot(
        attention,
        lax.all_gather(out_weight, "samp", axis=1, tiled=True),
        preferred_element_type=jnp.float32,
    )
    mixed = lax.psum_scatter(
        terms.astype(jnp.bfloat16), "head", scatter_dimension=1, tiled=True
    ).astype(jnp.float32)
    return mixed.astype(jnp.bfloat16).reshape(step_count, row_total, mixed.shape[1])


FIRST_VMEM = 60 * 1024 * 1024
VMEM = 24 * 1024 * 1024

CORE = [(0, 1), (1, 0), (2, 3), (3, 2)]
ACROSS_X = [(0, 2), (2, 0), (1, 3), (3, 1)]
INWARD = [(0, 1), (3, 2)]
MIDDLE = [(1, 2), (2, 1)]


def compiler_params(limit=VMEM):
    return pltpu.CompilerParams(vmem_limit_bytes=limit)


def small_cost():
    return pl.CostEstimate(flops=64, bytes_accessed=64, transcendentals=0)


def project(limit, here, states, weight, masks, cuts):
    features, width = weight.shape[0], weight.shape[1] // 4
    parts = [(low, high - low) for low, high in zip(cuts[:-1], cuts[1:])]

    def body(here_ref, state_any, weight_any, *rest):
        outs, (state, blocks, state_sems, block_sems) = rest[: 2 * len(parts)], rest[2 * len(parts) :]
        fetches, blocks_in = [], []
        for side in range(2):
            place = here_ref[2] ^ masks[side]
            columns = pl.ds(pl.multiple_of(place * width, width), width)
            blocks_in.append(
                pltpu.make_async_copy(
                    weight_any.at[:, columns], blocks.at[side], block_sems.at[side]
                )
            )
        for at, (low, rows) in enumerate(parts):
            fetches.append(
                pltpu.make_async_copy(
                    state_any.at[low : low + rows], state.at[low : low + rows], state_sems.at[at]
                )
            )
        blocks_in[0].start()
        fetches[0].start()
        blocks_in[1].start()
        for fetch in fetches[1:]:
            fetch.start()
        for at, (low, rows) in enumerate(parts):
            fetches[at].wait()
            for side in range(2):
                if at == 0:
                    blocks_in[side].wait()
                outs[side * len(parts) + at][...] = jnp.dot(
                    state[low : low + rows], blocks[side], preferred_element_type=jnp.float32
                ).astype(jnp.bfloat16)

    in_any = pl.BlockSpec(memory_space=pl.ANY)
    in_vmem = pl.BlockSpec(memory_space=pltpu.VMEM)
    outs = pl.pallas_call(
        body,
        in_specs=[pl.BlockSpec(memory_space=pltpu.SMEM), in_any, in_any],
        out_specs=[in_vmem] * (2 * len(parts)),
        out_shape=[jax.ShapeDtypeStruct((rows, width), jnp.bfloat16) for _, rows in parts] * 2,
        scratch_shapes=[
            pltpu.VMEM(states.shape, jnp.bfloat16),
            pltpu.VMEM((2, features, width), jnp.bfloat16),
            pltpu.SemaphoreType.DMA((len(parts),)),
            pltpu.SemaphoreType.DMA((2,)),
        ],
        compiler_params=compiler_params(limit),
        cost_estimate=small_cost(),
        name="project",
    )(here, states, weight)
    return outs[: len(parts)], outs[len(parts) :]


def attend(here, prompts, owners, lengths, queries, news, pages):
    steps, rows, width = queries.shape
    blocks = prompts.shape[0]
    block_rows = rows // blocks
    new_width = news.shape[2]
    groups = new_width // (2 * HD)
    sizes = [part.shape[0] for part in pages[0]]
    starts = [sum(sizes[:at]) for at in range(len(sizes))]
    tokens = sum(sizes)
    tiles = 4
    chunk = tokens // tiles
    flat = steps * block_rows
    factor = math.log2(math.e) / math.sqrt(HD)

    def body(here_ref, prompts_ref, owners_ref, lengths_ref, query_any, new_any, *rest):
        page_refs, rest = rest[: 4 * len(sizes)], rest[4 * len(sizes) :]
        out_ref, held, query_ref, new_ref, sems = rest
        plane = here_ref[1]

        def run(mine, used, length):
            query = query_ref[...].reshape(flat, width)
            new = new_ref[...].reshape(flat, new_width)
            shape = (GQA * flat, flat)
            asker = lax.broadcasted_iota(jnp.int32, shape, 0) % flat
            holder = lax.broadcasted_iota(jnp.int32, shape, 1)
            near_ok = jnp.logical_and(asker % block_rows == holder % block_rows, holder <= asker)
            last = (GQA * flat, chunk)
            last_ok = lax.broadcasted_iota(jnp.int32, last, 1) < length - (used - chunk)
            for group in range(groups):
                key = slice(2 * group * HD, (2 * group + 1) * HD)
                value = slice((2 * group + 1) * HD, (2 * group + 2) * HD)
                asked = jnp.concatenate(
                    [
                        query[:, (group * GQA + head) * HD : (group * GQA + head + 1) * HD]
                        for head in range(GQA)
                    ],
                    axis=0,
                )

                def scores(keys):
                    return lax.dot_general(
                        asked, keys, (((1,), (1,)), ((), ())), preferred_element_type=jnp.float32
                    )

                parts = [
                    scores(held[at * chunk : (at + 1) * chunk, key]) for at in range(used // chunk)
                ]
                parts[-1] = jnp.where(last_ok, parts[-1], masked_score)
                parts.append(jnp.where(near_ok, scores(new[:, key]), masked_score))
                peak = jnp.max(parts[0], axis=1, keepdims=True)
                for part in parts[1:]:
                    peak = jnp.maximum(peak, jnp.max(part, axis=1, keepdims=True))
                total, summed = 0.0, 0.0
                for at, part in enumerate(parts):
                    weights = jnp.exp2((part - peak) * factor)
                    total = total + jnp.sum(weights, axis=1, keepdims=True)
                    values = (
                        held[at * chunk : (at + 1) * chunk, value]
                        if at < len(parts) - 1
                        else new[:, value]
                    )
                    summed = summed + jnp.dot(
                        weights.astype(jnp.bfloat16), values, preferred_element_type=jnp.float32
                    )
                result = (summed / total).astype(jnp.bfloat16)
                for head in range(GQA):
                    column = (group * GQA + head) * HD
                    out_ref[:, mine, column : column + HD] = result[
                        head * flat : (head + 1) * flat
                    ].reshape(steps, block_rows, HD)

        @pl.loop(0, blocks)
        def _(block):
            mine = pl.ds(pl.multiple_of(block * block_rows, block_rows), block_rows)
            prompt = prompts_ref[block]
            slot, length = owners_ref[prompt], lengths_ref[prompt]
            fetch_query = pltpu.make_async_copy(query_any.at[:, mine], query_ref, sems.at[0])
            fetch_new = pltpu.make_async_copy(new_any.at[:, mine], new_ref, sems.at[1])
            fetch_query.start()
            fetch_new.start()
            for which, place in enumerate((plane, plane ^ 1, 3 - plane, (3 - plane) ^ 1)):

                @pl.when(slot == place)
                def _():
                    fetches = [
                        pltpu.make_async_copy(
                            page_refs[which * len(sizes) + at],
                            held.at[low : low + size],
                            sems.at[2 + at],
                        )
                        for at, (low, size) in enumerate(zip(starts, sizes))
                    ]
                    for fetch in fetches:
                        fetch.start()
                    for fetch in fetches:
                        fetch.wait()

            fetch_query.wait()
            fetch_new.wait()
            for count in range(1, tiles + 1):
                enough = length > (count - 1) * chunk
                if count < tiles:
                    enough = jnp.logical_and(enough, length <= count * chunk)

                @pl.when(enough)
                def _():
                    run(mine, count * chunk, length)

    in_vmem, in_smem, in_any = (
        pl.BlockSpec(memory_space=space) for space in (pltpu.VMEM, pltpu.SMEM, pl.ANY)
    )
    return pl.pallas_call(
        body,
        in_specs=[in_smem] * 4 + [in_any] * (2 + 4 * len(sizes)),
        out_specs=in_vmem,
        out_shape=jax.ShapeDtypeStruct(queries.shape, jnp.bfloat16),
        scratch_shapes=[
            pltpu.VMEM((tokens, new_width), jnp.bfloat16),
            pltpu.VMEM((steps, block_rows, width), jnp.bfloat16),
            pltpu.VMEM((steps, block_rows, new_width), jnp.bfloat16),
            pltpu.SemaphoreType.DMA((2 + len(sizes),)),
        ],
        compiler_params=compiler_params(),
        cost_estimate=small_cost(),
        name="attend",
    )(here, prompts, owners, lengths, queries, news, *[part for page in pages for part in page])


def spread(here, rows, own_weight, moved_weight):
    steps, count, features = rows.shape
    columns = own_weight.shape[1]
    tile = 256 if columns % 256 == 0 else columns

    def body(here_ref, row_ref, own_ref, moved_ref, keep_ref, send_ref):
        taken = row_ref[...].reshape(steps * count, features)
        keeps_own = (here_ref[1] ^ here_ref[2]) % 2 == 0
        for column in range(0, columns, tile):
            part = slice(column, column + tile)
            own = jnp.dot(taken, own_ref[:, part], preferred_element_type=jnp.float32)
            moved = jnp.dot(taken, moved_ref[:, part], preferred_element_type=jnp.float32)
            keep = jnp.where(keeps_own, own, moved).astype(jnp.bfloat16)
            send = jnp.where(keeps_own, moved, own).astype(jnp.bfloat16)
            keep_ref[:, :, part] = keep.reshape(steps, count, tile)
            send_ref[:, :, part] = send.reshape(steps, count, tile)

    in_vmem = pl.BlockSpec(memory_space=pltpu.VMEM)
    out_shape = jax.ShapeDtypeStruct((steps, count, columns), jnp.bfloat16)
    return pl.pallas_call(
        body,
        in_specs=[pl.BlockSpec(memory_space=pltpu.SMEM)] + [in_vmem] * 3,
        out_specs=[in_vmem, in_vmem],
        out_shape=[out_shape, out_shape],
        compiler_params=compiler_params(),
        cost_estimate=small_cost(),
        name="spread",
    )(here, rows, own_weight, moved_weight)


def run_small(body, name, here, operands, out_shape):
    in_vmem = pl.BlockSpec(memory_space=pltpu.VMEM)
    return pl.pallas_call(
        body,
        in_specs=[pl.BlockSpec(memory_space=pltpu.SMEM)] + [in_vmem] * len(operands),
        out_specs=in_vmem,
        out_shape=jax.ShapeDtypeStruct(out_shape, jnp.bfloat16),
        compiler_params=compiler_params(),
        cost_estimate=small_cost(),
        name=name,
    )(here, *operands)


def added(here, *parts):
    def body(_, *refs):
        total = refs[0][...].astype(jnp.float32)
        for ref in refs[1:-1]:
            total = total + ref[...].astype(jnp.float32)
        refs[-1][...] = total.astype(jnp.bfloat16)

    return run_small(body, "added", here, parts, parts[0].shape)


def added_half(here, mine, wide, *narrow):
    half = wide[0].shape[0] // 2

    def body(here_ref, *refs):
        chip = here_ref[2] // 2
        steps = pl.ds((chip if mine else 1 - chip) * half, half)
        total = refs[0][steps].astype(jnp.float32)
        for at, ref in enumerate(refs[1:-1], 1):
            part = ref[steps] if at < len(wide) else ref[...]
            total = total + part.astype(jnp.float32)
        refs[-1][...] = total.astype(jnp.bfloat16)

    shape = (half, *wide[0].shape[1:])
    return run_small(body, "added_half", here, (*wide, *narrow), shape)


def after(value, *others):
    return lax.optimization_barrier((value, *others))[0]


def sent_home(value, target):
    same, turned = [], []
    for source in (1, 2):
        side = source // 2
        for at in range(2):
            goal = target(source) * 4 + 2 * side + at
            same.append((source * 4 + 2 * side + at, goal))
            turned.append((source * 4 + 2 * (1 - side) + at, goal))
    return [lax.ppermute(value, ("samp", "head"), pairs) for pairs in (same, turned)]


def across_home(value):
    pairs = [
        (source * 4 + 2 * (1 - source // 2) + at, source * 4 + 2 * (source // 2) + at)
        for source in (1, 2)
        for at in range(2)
    ]
    return lax.ppermute(value, ("samp", "head"), pairs)


def inward_plan(
    prompt_states,
    prompt_lengths,
    prompt_owner,
    kv_weight,
    sampler_prompts,
    step_queries,
    step_kv,
    out_weight,
):
    group, plane, head = (lax.axis_index(name) for name in ("groups", "samp", "head"))
    chip = head // 2
    here = jnp.stack([group, plane, head]).astype(jnp.int32)

    def on_samp(value, pairs):
        return lax.ppermute(value, "samp", pairs)

    def on_head(value, pairs):
        return lax.ppermute(value, "head", pairs)

    half = out_weight.shape[0] // 2
    cut = half * 7 // 10

    def weight_part(low, size, *others):
        part = lax.dynamic_slice_in_dim(after(out_weight, *others), group * half + low, size, 0)
        return on_samp(part, INWARD)

    weight_first = weight_part(0, cut)
    end_news = on_samp(step_kv, INWARD)

    states = prompt_states[0]
    tokens = states.shape[0]
    cuts = [0, tokens * 3 // 8, tokens]
    sent, kept = project(FIRST_VMEM, here, states, kv_weight, (3, 2), cuts)
    leaving_first = added(here, kept[0], on_head(sent[0], CORE))
    leaving_second = added(here, kept[1], after(on_head(sent[1], CORE), leaving_first))
    crossed_first = on_head(leaving_first, ACROSS_X)
    crossed_second = on_head(leaving_second, ACROSS_X)
    sent, kept = project(
        VMEM, here, after(states, leaving_first, leaving_second), kv_weight, (1, 0), cuts
    )
    sent = [on_head(value, CORE) for value in sent]
    first = added(here, after(kept[0], end_news), sent[0], crossed_first)
    end_first = on_samp(after(first, weight_first), INWARD)
    far_first = on_samp(first, MIDDLE)
    far_end_first = on_samp(end_first, MIDDLE)
    second = added(here, kept[1], after(sent[1], far_first, far_end_first), crossed_second)
    end_second = on_samp(second, INWARD)
    far_second = on_samp(second, MIDDLE)
    moved_first = lax.ppermute(weight_first, "groups", [(0, 1), (1, 0)])
    far_end_second = on_samp(after(end_second, far_second, moved_first), MIDDLE)
    pages = (
        (first, second),
        (end_first, end_second),
        (far_first, far_second),
        (far_end_first, far_end_second),
    )
    weight_second = weight_part(cut, half - cut, end_second)

    def attended(prompts, queries, news):
        return attend(here, prompts, prompt_owner, prompt_lengths, queries, news, pages)

    end_prompts = on_samp(after(sampler_prompts, second), INWARD)
    end_queries = on_samp(after(step_queries, weight_second), INWARD)
    moved_second = lax.ppermute(weight_second, "groups", [(0, 1), (1, 0)])
    mine = jnp.concatenate([weight_first, weight_second], axis=0)
    other = jnp.concatenate([moved_first, moved_second], axis=0)
    moved_weight = jnp.where(
        group == 0,
        jnp.concatenate([mine, other], axis=0),
        jnp.concatenate([other, mine], axis=0),
    )

    def spread_out(rows):
        keep, send = spread(here, rows, out_weight, moved_weight)
        return keep, on_head(send, CORE)

    own_rows = attended(sampler_prompts, after(step_queries, weight_second), step_kv)
    far_own_rows = on_samp(own_rows, MIDDLE)
    own_keep, own_arrived = spread_out(own_rows)
    end_rows = attended(end_prompts, after(end_queries, own_keep), end_news)
    far_end_rows = on_samp(end_rows, MIDDLE)
    own_chip = added(here, own_keep, after(own_arrived, end_rows))
    own_crossed = across_home(own_chip)
    far_keep, far_arrived = spread_out(after(far_own_rows, own_chip))
    end_keep, end_arrived = spread_out(after(end_rows, far_keep))
    far_leaving = added_half(here, False, (far_keep, after(far_arrived, end_keep)))
    far_crossed = on_head(far_leaving, ACROSS_X)
    end_leaving = added_half(here, False, (end_keep, after(end_arrived, far_leaving)))
    end_crossed = on_head(end_leaving, ACROSS_X)
    own_home = added(here, own_chip, after(own_crossed, end_leaving))
    beyond_keep, beyond_arrived = spread_out(after(far_end_rows, own_home))
    beyond_leaving = added_half(here, False, (beyond_keep, beyond_arrived))
    beyond_crossed = on_head(beyond_leaving, ACROSS_X)
    far_sum = added_half(here, True, (far_keep, after(far_arrived, beyond_leaving)), far_crossed)
    far_home = sent_home(far_sum, lambda at: 3 - at)
    end_sum = added_half(here, True, (end_keep, after(end_arrived, far_sum)), end_crossed)
    end_home = sent_home(end_sum, lambda at: at ^ 1)
    beyond_sum = added_half(
        here, True, (beyond_keep, after(beyond_arrived, *far_home)), beyond_crossed
    )
    beyond_home = sent_home(beyond_sum, lambda at: (3 - at) ^ 1)

    is_middle = jnp.logical_or(plane == 1, plane == 2)
    near_side = chip == plane // 2
    straight, turned = (
        jnp.where(is_middle, far_home[which], jnp.where(near_side, end_home[which], beyond_home[which]))
        for which in range(2)
    )
    return jnp.where(
        jnp.logical_and(is_middle, near_side),
        own_home,
        jnp.where(
            chip == 0,
            jnp.concatenate([straight, turned], axis=0),
            jnp.concatenate([turned, straight], axis=0),
        ),
    )


def solution(mesh):
    line, width = mesh.shape["samp"], mesh.shape["head"]
    paired = line == 4 and width == 4 and mesh.shape["groups"] == 2
    on_device = inward_plan if paired else general_plan

    placed = (
        P(("groups", "samp"), None, "head"),
        P("groups"),
        P("groups"),
        P("head", None),
        P(("groups", "samp")),
        P(None, ("groups", "samp"), "head"),
        P(None, ("groups", "samp"), "head"),
        P("head", "samp"),
    )
    return jax.shard_map(
        on_device,
        mesh=mesh,
        in_specs=placed,
        out_specs=P(None, ("groups", "samp"), "head"),
        check_vma=False,
    )
```

```python
import math

import jax
import jax.numpy as jnp
from jax import lax
from jax.experimental import pallas as pl
from jax.experimental.pallas import tpu as pltpu
from jax.sharding import PartitionSpec as P

HD = 128
GQA = 5


masked_score = -1e30


def prompt_partial(queries, page_block, length):
    row_count = queries.shape[0]
    groups = page_block.shape[0] // (2 * HD)
    score_scale = 1.0 / math.sqrt(HD)
    query_heads = queries.reshape(row_count, groups, GQA, HD)
    page_heads = page_block.reshape(groups, 2, HD, page_block.shape[1])
    scores = (
        jnp.einsum(
            "rgjd,gdl->grjl", query_heads, page_heads[:, 0], preferred_element_type=jnp.float32
        )
        * score_scale
    )
    usable = lax.broadcasted_iota(jnp.int32, scores.shape, 3) < length
    peak_score = jnp.max(jnp.where(usable, scores, masked_score), axis=3)
    weights = jnp.where(usable, jnp.exp(scores - peak_score[..., None]), 0.0)
    totals = jnp.sum(weights, axis=3)
    summed = jnp.einsum(
        "grjl,gdl->grjd",
        weights.astype(jnp.bfloat16),
        page_heads[:, 1],
        preferred_element_type=jnp.float32,
    )
    summed = jnp.transpose(summed, (1, 0, 2, 3)).reshape(row_count, groups * GQA * HD)
    peak_score = jnp.transpose(peak_score, (1, 0, 2)).reshape(row_count, groups * GQA)
    totals = jnp.transpose(totals, (1, 0, 2)).reshape(row_count, groups * GQA)
    return (summed, peak_score, totals)


def general_plan(
    prompt_states,
    prompt_lengths,
    prompt_owner,
    kv_weight,
    sampler_prompts,
    step_queries,
    step_kv,
    out_weight,
):
    states = prompt_states[0]
    own_pages = lax.psum_scatter(
        lax.dot_general(
            kv_weight, states, (((0,), (1,)), ((), ())), preferred_element_type=jnp.float32
        ).astype(jnp.bfloat16),
        "head",
        scatter_dimension=0,
        tiled=True,
    )
    step_count = step_queries.shape[0]
    row_total = step_queries.shape[1]
    prompt_count = sampler_prompts.shape[0]
    block_rows = row_total // prompt_count
    head_width = step_queries.shape[2]
    groups = own_pages.shape[0] // (2 * HD)
    owner_slots = jnp.take(prompt_owner, sampler_prompts)
    block_lengths = jnp.take(prompt_lengths, sampler_prompts)
    block_queries = [
        step_queries[:, position * block_rows : (position + 1) * block_rows].reshape(
            step_count * block_rows, head_width
        )
        for position in range(prompt_count)
    ]
    library = lax.all_gather(own_pages[None], "samp", axis=0, tiled=True)
    partials = []
    for position in range(prompt_count):
        page_block = lax.dynamic_index_in_dim(library, owner_slots[position], 0, keepdims=False)
        partials.append(
            prompt_partial(block_queries[position], page_block, block_lengths[position])
        )
    prompt_sum = jnp.concatenate(
        [entry[0].reshape(step_count, block_rows, groups, GQA, HD) for entry in partials], axis=1
    )
    prompt_peak = jnp.concatenate(
        [entry[1].reshape(step_count, block_rows, groups, GQA) for entry in partials], axis=1
    )
    prompt_total = jnp.concatenate(
        [entry[2].reshape(step_count, block_rows, groups, GQA) for entry in partials], axis=1
    )
    score_scale = 1.0 / math.sqrt(HD)
    query_all = step_queries.reshape(step_count, row_total, groups, GQA, HD)
    own_cache = step_kv.reshape(step_count, row_total, groups, 2, HD)
    near_scores = (
        jnp.einsum(
            "trgjd,urgd->trgju",
            query_all,
            own_cache[:, :, :, 0],
            preferred_element_type=jnp.float32,
        )
        * score_scale
    )
    causal = lax.broadcasted_iota(jnp.int32, near_scores.shape, 4) <= lax.broadcasted_iota(
        jnp.int32, near_scores.shape, 0
    )
    near_peak = jnp.max(jnp.where(causal, near_scores, masked_score), axis=4)
    near_weights = jnp.where(causal, jnp.exp(near_scores - near_peak[..., None]), 0.0)
    near_total = jnp.sum(near_weights, axis=4)
    near_sum = jnp.einsum(
        "trgju,urgd->trgjd",
        near_weights.astype(jnp.bfloat16),
        own_cache[:, :, :, 1],
        preferred_element_type=jnp.float32,
    )
    peak_all = jnp.maximum(prompt_peak, near_peak)
    far_factor = jnp.exp(prompt_peak - peak_all)
    near_factor = jnp.exp(near_peak - peak_all)
    numerator = prompt_sum * far_factor[..., None] + near_sum * near_factor[..., None]
    denominator = prompt_total * far_factor + near_total * near_factor
    attention = (numerator / denominator[..., None]).astype(jnp.bfloat16)
    attention = attention.reshape(step_count * row_total, groups * GQA * HD)
    terms = jnp.dot(
        attention,
        lax.all_gather(out_weight, "samp", axis=1, tiled=True),
        preferred_element_type=jnp.float32,
    )
    mixed = lax.psum_scatter(
        terms.astype(jnp.bfloat16), "head", scatter_dimension=1, tiled=True
    ).astype(jnp.float32)
    return mixed.astype(jnp.bfloat16).reshape(step_count, row_total, mixed.shape[1])


VMEM = 24 * 1024 * 1024
LARGE_VMEM = 60 * 1024 * 1024

CORE = [(0, 1), (1, 0), (2, 3), (3, 2)]
ACROSS_X = [(0, 2), (2, 0), (1, 3), (3, 1)]
INWARD = [(0, 1), (3, 2)]
MIDDLE = [(1, 2), (2, 1)]


def compiler_params(limit=VMEM):
    return pltpu.CompilerParams(vmem_limit_bytes=limit)


def small_cost():
    return pl.CostEstimate(flops=64, bytes_accessed=64, transcendentals=0)


def project(here, states, weight, masks, cuts):
    features, width = weight.shape[0], weight.shape[1] // 4
    parts = [(low, high - low) for low, high in zip(cuts[:-1], cuts[1:])]

    def body(here_ref, state_hbm, weight_hbm, *rest):
        outs, (state, blocks, state_sems, block_sems) = rest[: 2 * len(parts)], rest[2 * len(parts) :]
        fetches, blocks_in = [], []
        for side in range(2):
            place = here_ref[2] ^ masks[side]
            columns = pl.ds(pl.multiple_of(place * width, width), width)
            blocks_in.append(
                pltpu.make_async_copy(
                    weight_hbm.at[:, columns], blocks.at[side], block_sems.at[side]
                )
            )
        for at, (low, rows) in enumerate(parts):
            fetches.append(
                pltpu.make_async_copy(
                    state_hbm.at[low : low + rows], state.at[low : low + rows], state_sems.at[at]
                )
            )
        blocks_in[0].start()
        fetches[0].start()
        blocks_in[1].start()
        for fetch in fetches[1:]:
            fetch.start()
        for at, (low, rows) in enumerate(parts):
            fetches[at].wait()
            for side in range(2):
                if at == 0:
                    blocks_in[side].wait()
                outs[side * len(parts) + at][...] = jnp.dot(
                    state[low : low + rows], blocks[side], preferred_element_type=jnp.float32
                ).astype(jnp.bfloat16)

    in_hbm = pl.BlockSpec(memory_space=pltpu.HBM)
    in_vmem = pl.BlockSpec(memory_space=pltpu.VMEM)
    outs = pl.pallas_call(
        body,
        in_specs=[pl.BlockSpec(memory_space=pltpu.SMEM), in_hbm, in_hbm],
        out_specs=[in_vmem] * (2 * len(parts)),
        out_shape=[jax.ShapeDtypeStruct((rows, width), jnp.bfloat16) for _, rows in parts] * 2,
        scratch_shapes=[
            pltpu.VMEM(states.shape, jnp.bfloat16),
            pltpu.VMEM((2, features, width), jnp.bfloat16),
            pltpu.SemaphoreType.DMA((len(parts),)),
            pltpu.SemaphoreType.DMA((2,)),
        ],
        compiler_params=compiler_params(LARGE_VMEM),
        cost_estimate=small_cost(),
        name="project",
    )(here, states, weight)
    return outs[: len(parts)], outs[len(parts) :]


def attend(chosen, here, prompts, owners, lengths, queries, news, pages):
    news, new_start = news
    steps, rows, _ = queries.shape
    blocks = prompts.shape[0]
    block_rows = rows // blocks
    new_width = pages[0][0].shape[1]
    groups = new_width // (2 * HD)
    width = groups * GQA * HD
    tokens = sum(part.shape[0] for part in pages[0])
    most = max(len(page) for page in pages)
    page_parts = [part for page in pages for part in page]
    tiles = 4
    chunk = tokens // tiles
    flat = steps * block_rows
    factor = math.log2(math.e) / math.sqrt(HD)

    def body(here_ref, prompts_ref, owners_ref, lengths_ref, query_hbm, new_hbm, *rest):
        page_refs, rest = rest[: len(page_parts)], rest[len(page_parts) :]
        out_ref, held, query_ref, new_ref, sems = rest
        plane = here_ref[1]

        def run(written, used, length):
            query = query_ref[...].reshape(flat, width)
            new = new_ref[...].reshape(flat, new_width)
            shape = (GQA * flat, flat)
            asker = lax.broadcasted_iota(jnp.int32, shape, 0) % flat
            holder = lax.broadcasted_iota(jnp.int32, shape, 1)
            near_ok = jnp.logical_and(asker % block_rows == holder % block_rows, holder <= asker)
            last = (GQA * flat, chunk)
            last_ok = lax.broadcasted_iota(jnp.int32, last, 1) < length - (used - chunk)
            for group in range(groups):
                key = slice(2 * group * HD, (2 * group + 1) * HD)
                value = slice((2 * group + 1) * HD, (2 * group + 2) * HD)
                asked = jnp.concatenate(
                    [
                        query[:, (group * GQA + head) * HD : (group * GQA + head + 1) * HD]
                        for head in range(GQA)
                    ],
                    axis=0,
                )

                def scores(keys):
                    return lax.dot_general(
                        asked, keys, (((1,), (1,)), ((), ())), preferred_element_type=jnp.float32
                    )

                parts = [
                    scores(held[at * chunk : (at + 1) * chunk, key]) for at in range(used // chunk)
                ]
                parts[-1] = jnp.where(last_ok, parts[-1], masked_score)
                parts.append(jnp.where(near_ok, scores(new[:, key]), masked_score))
                peak = jnp.max(parts[0], axis=1, keepdims=True)
                for part in parts[1:]:
                    peak = jnp.maximum(peak, jnp.max(part, axis=1, keepdims=True))
                total, summed = 0.0, 0.0
                for at, part in enumerate(parts):
                    weights = jnp.exp2((part - peak) * factor)
                    total = total + jnp.sum(weights, axis=1, keepdims=True)
                    values = (
                        held[at * chunk : (at + 1) * chunk, value]
                        if at < len(parts) - 1
                        else new[:, value]
                    )
                    summed = summed + jnp.dot(
                        weights.astype(jnp.bfloat16), values, preferred_element_type=jnp.float32
                    )
                result = (summed / total).astype(jnp.bfloat16)
                for head in range(GQA):
                    column = (group * GQA + head) * HD
                    out_ref[:, written, column : column + HD] = result[
                        head * flat : (head + 1) * flat
                    ].reshape(steps, block_rows, HD)

        @pl.loop(*chosen)
        def _(block):
            mine = pl.ds(pl.multiple_of(block * block_rows, block_rows), block_rows)
            written = pl.ds(
                pl.multiple_of((block - chosen[0]) * block_rows, block_rows), block_rows
            )
            prompt = prompts_ref[block]
            slot, length = owners_ref[prompt], lengths_ref[prompt]
            fetch_query = pltpu.make_async_copy(query_hbm.at[:, mine, :width], query_ref, sems.at[0])
            fetch_new = pltpu.make_async_copy(new_hbm.at[:, mine, new_start : new_start + new_width], new_ref, sems.at[1])
            fetch_query.start()
            fetch_new.start()
            passed = 0
            for page, place in zip(pages, (plane, plane ^ 1, 3 - plane, (3 - plane) ^ 1)):
                refs = page_refs[passed : passed + len(page)]
                passed += len(page)

                @pl.when(slot == place)
                def _():
                    low, fetches = 0, []
                    for at, ref in enumerate(refs):
                        target = held.at[low : low + ref.shape[0]]
                        fetches.append(pltpu.make_async_copy(ref, target, sems.at[2 + at]))
                        low += ref.shape[0]
                    for fetch in fetches:
                        fetch.start()
                    for fetch in fetches:
                        fetch.wait()

            fetch_query.wait()
            fetch_new.wait()
            for count in range(1, tiles + 1):
                enough = length > (count - 1) * chunk
                if count < tiles:
                    enough = jnp.logical_and(enough, length <= count * chunk)

                @pl.when(enough)
                def _():
                    run(written, count * chunk, length)

    in_vmem, in_smem, in_hbm = (
        pl.BlockSpec(memory_space=space) for space in (pltpu.VMEM, pltpu.SMEM, pltpu.HBM)
    )
    return pl.pallas_call(
        body,
        in_specs=[in_smem] * 4 + [in_hbm] * (2 + len(page_parts)),
        out_specs=in_vmem,
        out_shape=jax.ShapeDtypeStruct(
            (steps, (chosen[1] - chosen[0]) * block_rows, width), jnp.bfloat16
        ),
        scratch_shapes=[
            pltpu.VMEM((tokens, new_width), jnp.bfloat16),
            pltpu.VMEM((steps, block_rows, width), jnp.bfloat16),
            pltpu.VMEM((steps, block_rows, new_width), jnp.bfloat16),
            pltpu.SemaphoreType.DMA((2 + most,)),
        ],
        compiler_params=compiler_params(LARGE_VMEM),
        cost_estimate=small_cost(),
        name="attend",
    )(here, prompts, owners, lengths, queries, news, *page_parts)


def spread(here, blocks, own_weight, moved_weights):
    count, moved_count = len(blocks), len(moved_weights)
    steps, _, features = blocks[0].shape
    columns = own_weight.shape[1]
    tile = 256 if columns % 256 == 0 else columns
    ends = [0]
    for block in blocks:
        ends.append(ends[-1] + block.shape[1])
    places = [slice(low, high) for low, high in zip(ends[:-1], ends[1:])]

    def body(here_ref, *refs):
        row_refs, own_ref, refs = refs[:count], refs[count], refs[count + 1 :]
        moved_refs, (keep_ref, send_ref, taken_ref) = refs[:moved_count], refs[moved_count:]
        for ref, place in zip(row_refs, places):
            flat = slice(steps * place.start, steps * place.stop)
            taken_ref[flat] = ref[...].reshape(flat.stop - flat.start, features)
        taken = taken_ref[...]
        pieces = []
        for low, other, part in moved_weights:
            start = (here_ref[0] ^ other) * (features // 2) + low
            pieces.append(taken_ref[:, pl.ds(pl.multiple_of(start, 128), part.shape[0])])
        keeps_own = (here_ref[1] ^ here_ref[2]) % 2 == 0
        for column in range(0, columns, tile):
            part = slice(column, column + tile)
            own = jnp.dot(taken, own_ref[:, part], preferred_element_type=jnp.float32)
            moved = 0.0
            for piece, moved_ref in zip(pieces, moved_refs):
                moved = moved + jnp.dot(
                    piece, moved_ref[:, part], preferred_element_type=jnp.float32
                )
            keep = jnp.where(keeps_own, own, moved).astype(jnp.bfloat16)
            send = jnp.where(keeps_own, moved, own).astype(jnp.bfloat16)
            for place in places:
                flat = slice(steps * place.start, steps * place.stop)
                shape = (steps, place.stop - place.start, tile)
                keep_ref[:, place, part] = keep[flat].reshape(shape)
                send_ref[:, place, part] = send[flat].reshape(shape)

    in_vmem = pl.BlockSpec(memory_space=pltpu.VMEM)
    out_shape = jax.ShapeDtypeStruct((steps, ends[-1], columns), jnp.bfloat16)
    return pl.pallas_call(
        body,
        in_specs=[pl.BlockSpec(memory_space=pltpu.SMEM)] + [in_vmem] * (count + 1 + moved_count),
        out_specs=[in_vmem, in_vmem],
        out_shape=[out_shape, out_shape],
        scratch_shapes=[pltpu.VMEM((steps * ends[-1], features), jnp.bfloat16)],
        compiler_params=compiler_params(),
        cost_estimate=small_cost(),
        name="spread",
    )(here, *blocks, own_weight, *[part for _, _, part in moved_weights])


def run_small(body, name, here, operands, out_shape, outs=1):
    in_vmem = pl.BlockSpec(memory_space=pltpu.VMEM)
    return pl.pallas_call(
        body,
        in_specs=[pl.BlockSpec(memory_space=pltpu.SMEM)] + [in_vmem] * len(operands),
        out_specs=[in_vmem] * outs,
        out_shape=[jax.ShapeDtypeStruct(out_shape, jnp.bfloat16)] * outs,
        compiler_params=compiler_params(),
        cost_estimate=small_cost(),
        name=name,
    )(here, *operands)


def added(here, *parts):
    def body(_, *refs):
        total = refs[0][...].astype(jnp.float32)
        for ref in refs[1:-1]:
            total = total + ref[...].astype(jnp.float32)
        refs[-1][...] = total.astype(jnp.bfloat16)

    return run_small(body, "added", here, parts, parts[0].shape)[0]


def stacked(here, *parts):
    rows = [part.shape[0] for part in parts]

    def body(_, *refs):
        for at, ref in enumerate(refs[:-1]):
            refs[-1][sum(rows[:at]) : sum(rows[: at + 1])] = ref[...]

    return run_small(body, "stacked", here, parts, (sum(rows), *parts[0].shape[1:]))[0]


def added_half(here, mine, wide, narrow=(), pieces=1):
    steps, rows, columns = wide[0].shape
    half, piece = steps // 2, rows // pieces

    def body(here_ref, *refs):
        ins, outs = refs[:-pieces], refs[-pieces:]
        chip = here_ref[2] // 2
        taken = pl.ds((chip if mine else 1 - chip) * half, half)
        total = ins[0][taken].astype(jnp.float32)
        for at, ref in enumerate(ins[1:], 1):
            part = ref[taken] if at < len(wide) else ref[...]
            total = total + part.astype(jnp.float32)
        total = total.astype(jnp.bfloat16)
        for at, out in enumerate(outs):
            out[...] = total[:, at * piece : (at + 1) * piece]

    outs = run_small(body, "added_half", here, (*wide, *narrow), (half, piece, columns), pieces)
    return outs if pieces > 1 else outs[0]


def added_halves(here, one, two, far_crossed, end_crossed):
    steps, rows, columns = one.shape
    half, piece = steps // 2, rows // 2

    def body(here_ref, one_ref, two_ref, far_ref, end_ref, first_ref, second_ref):
        chip = here_ref[2] // 2
        taken = pl.ds(chip * half, half)
        total = one_ref[taken].astype(jnp.float32) + two_ref[taken].astype(jnp.float32)
        far = (total[:, :piece] + far_ref[...].astype(jnp.float32)).astype(jnp.bfloat16)
        end = (total[:, piece:] + end_ref[...].astype(jnp.float32)).astype(jnp.bfloat16)
        at_home = here_ref[1] // 2 == chip

        @pl.when(at_home)
        def _():
            first_ref[...] = far
            second_ref[...] = end

        @pl.when(jnp.logical_not(at_home))
        def _():
            first_ref[...] = end
            second_ref[...] = far

    shape = (half, piece, columns)
    return run_small(body, "added_halves", here, (one, two, far_crossed, end_crossed), shape, 2)


def after(value, *others):
    return lax.optimization_barrier((value, *others))[0]


def home_pairs(target, turned):
    pairs = []
    for source in (1, 2):
        side = source // 2
        chip = 1 - side if turned else side
        for at in range(2):
            pairs.append((source * 4 + 2 * chip + at, target(source) * 4 + 2 * side + at))
    return pairs


def sent_home(value, *pairs):
    return lax.ppermute(value, ("samp", "head"), [pair for part in pairs for pair in part])


def across_home(value):
    pairs = [
        (source * 4 + 2 * (1 - source // 2) + at, source * 4 + 2 * (source // 2) + at)
        for source in (1, 2)
        for at in range(2)
    ]
    return lax.ppermute(value, ("samp", "head"), pairs)


def inward_plan(
    prompt_states,
    prompt_lengths,
    prompt_owner,
    kv_weight,
    sampler_prompts,
    step_queries,
    step_kv,
    out_weight,
):
    group, plane, head = (lax.axis_index(name) for name in ("groups", "samp", "head"))
    chip = head // 2
    here = jnp.stack([group, plane, head]).astype(jnp.int32)

    def on_samp(value, pairs):
        return lax.ppermute(value, "samp", pairs)

    def on_head(value, pairs):
        return lax.ppermute(value, "head", pairs)

    states = prompt_states[0]
    tokens = states.shape[0]
    cuts = [0, tokens * 3 // 8, tokens]
    sent, kept = project(here, states, kv_weight, (3, 2), cuts)

    half = out_weight.shape[0] // 2
    weight_cuts = [0, half * 2 // 5, half * 3 // 5, half]

    def weight_part(at, *others):
        low, size = weight_cuts[at], weight_cuts[at + 1] - weight_cuts[at]
        part = lax.dynamic_slice_in_dim(after(out_weight, *others), group * half + low, size, 0)
        return on_samp(part, INWARD)

    def swapped(part):
        return lax.ppermute(part, "groups", [(0, 1), (1, 0)])

    weight_0 = weight_part(0, sent[0])
    leaving_first = added(here, kept[0], on_head(sent[0], CORE))
    leaving_second = added(here, kept[1], after(on_head(sent[1], CORE), leaving_first))
    crossed_first = on_head(leaving_first, ACROSS_X)
    crossed_second = on_head(leaving_second, ACROSS_X)
    sent, kept = project(
        here, after(states, leaving_first, leaving_second), kv_weight, (1, 0), cuts
    )
    sent = [on_head(value, CORE) for value in sent]
    first = added(here, kept[0], sent[0], crossed_first)
    end_first = on_samp(after(first, weight_0), INWARD)
    far_first = on_samp(first, MIDDLE)
    second = added(here, kept[1], after(sent[1], far_first, end_first), crossed_second)
    end_second = on_samp(second, INWARD)
    far_second = on_samp(second, MIDDLE)
    end_page = stacked(here, end_first, end_second)
    far_end_page = on_samp(after(end_page, far_second), MIDDLE)
    pages = ((first, second), (end_page,), (far_first, far_second), (far_end_page,))
    end_prompts = on_samp(after(sampler_prompts, second), INWARD)
    weight_1, weight_2 = (weight_part(at, end_second, end_prompts) for at in (1, 2))
    asked = jnp.concatenate([after(step_queries, first), step_kv], axis=2)
    end_asked = on_samp(after(asked, weight_1, weight_2), INWARD)
    moved_0, moved_1, moved_2 = swapped(weight_0), swapped(weight_1), swapped(weight_2)
    parts = ((weight_0, moved_0), (weight_1, moved_1), (weight_2, moved_2))
    moved_weights = [
        (low, side, part[side]) for side in range(2) for low, part in zip(weight_cuts, parts)
    ]

    def hopped(*values):
        token = here
        for value in values:
            token = on_head(after(token, value), CORE)
        return token

    def attended(place, chosen, prompts, queries, news):
        rows = attend(
            chosen, place, prompts, prompt_owner, prompt_lengths, queries, news, pages
        )
        return rows, on_samp(rows, MIDDLE)

    def spread_out(*blocks, place=here):
        keep, send = spread(place, blocks, out_weight, moved_weights)
        return keep, on_head(send, CORE)

    blocks = sampler_prompts.shape[0]
    own_rows, far_own_rows = attended(
        here, (0, blocks), sampler_prompts, after(step_queries, moved_0), (step_kv, 0)
    )
    end_rows, far_end_rows = attended(
        here,
        (0, blocks),
        end_prompts,
        after(end_asked, own_rows),
        (end_asked, step_queries.shape[2]),
    )
    both_keep, both_arrived = spread_out(far_own_rows, end_rows)
    far_leaving, end_leaving = added_half(here, False, (both_keep, both_arrived), (), 2)
    end_crossed = on_head(end_leaving, ACROSS_X)
    far_crossed = on_head(far_leaving, ACROSS_X)
    own_keep, own_arrived = spread_out(own_rows, place=hopped(end_leaving, end_leaving))
    own_chip = added(here, own_keep, own_arrived)
    own_crossed = across_home(own_chip)
    beyond_keep, beyond_arrived = spread_out(
        far_end_rows, place=hopped(far_end_rows, far_end_rows, own_chip, end_crossed)
    )
    beyond_leaving = added_half(here, False, (beyond_keep, beyond_arrived))
    beyond_crossed = on_head(beyond_leaving, ACROSS_X)
    first_sum, second_sum = added_halves(
        hopped(beyond_leaving), both_keep, both_arrived, far_crossed, end_crossed
    )

    def far(at):
        return 3 - at

    def end(at):
        return at ^ 1

    def beyond(at):
        return (3 - at) ^ 1

    first_home = sent_home(first_sum, home_pairs(far, False), home_pairs(end, True))
    second_home = sent_home(second_sum, home_pairs(far, True), home_pairs(end, False))
    beyond_sum = added_half(
        hopped(beyond_crossed),
        True,
        (beyond_keep, after(beyond_arrived, first_home, second_home)),
        (beyond_crossed,),
    )
    beyond_home = [sent_home(beyond_sum, home_pairs(beyond, turned)) for turned in (False, True)]
    own_home = added(here, own_chip, after(own_crossed, beyond_sum))

    is_middle = jnp.logical_or(plane == 1, plane == 2)
    near_side = chip == plane // 2
    straight = jnp.where(is_middle, first_home, jnp.where(near_side, second_home, beyond_home[0]))
    turned = jnp.where(is_middle, second_home, jnp.where(near_side, first_home, beyond_home[1]))
    return jnp.where(
        jnp.logical_and(is_middle, near_side),
        own_home,
        jnp.where(
            chip == 0,
            jnp.concatenate([straight, turned], axis=0),
            jnp.concatenate([turned, straight], axis=0),
        ),
    )


def solution(mesh):
    line, width = mesh.shape["samp"], mesh.shape["head"]
    paired = line == 4 and width == 4 and mesh.shape["groups"] == 2
    on_device = inward_plan if paired else general_plan

    placed = (
        P(("groups", "samp"), None, "head"),
        P("groups"),
        P("groups"),
        P("head", None),
        P(("groups", "samp")),
        P(None, ("groups", "samp"), "head"),
        P(None, ("groups", "samp"), "head"),
        P("head", "samp"),
    )
    return jax.shard_map(
        on_device,
        mesh=mesh,
        in_specs=placed,
        out_specs=P(None, ("groups", "samp"), "head"),
        check_vma=False,
    )
```

```python
import math

import jax
import jax.numpy as jnp
from jax import lax
from jax.experimental import pallas as pl
from jax.experimental.pallas import tpu as pltpu
from jax.sharding import PartitionSpec as P

HD = 128
GQA = 5


masked_score = -1e30


def prompt_partial(queries, page_block, length):
    row_count = queries.shape[0]
    groups = page_block.shape[0] // (2 * HD)
    score_scale = 1.0 / math.sqrt(HD)
    query_heads = queries.reshape(row_count, groups, GQA, HD)
    page_heads = page_block.reshape(groups, 2, HD, page_block.shape[1])
    scores = (
        jnp.einsum(
            "rgjd,gdl->grjl", query_heads, page_heads[:, 0], preferred_element_type=jnp.float32
        )
        * score_scale
    )
    usable = lax.broadcasted_iota(jnp.int32, scores.shape, 3) < length
    peak_score = jnp.max(jnp.where(usable, scores, masked_score), axis=3)
    weights = jnp.where(usable, jnp.exp(scores - peak_score[..., None]), 0.0)
    totals = jnp.sum(weights, axis=3)
    summed = jnp.einsum(
        "grjl,gdl->grjd",
        weights.astype(jnp.bfloat16),
        page_heads[:, 1],
        preferred_element_type=jnp.float32,
    )
    summed = jnp.transpose(summed, (1, 0, 2, 3)).reshape(row_count, groups * GQA * HD)
    peak_score = jnp.transpose(peak_score, (1, 0, 2)).reshape(row_count, groups * GQA)
    totals = jnp.transpose(totals, (1, 0, 2)).reshape(row_count, groups * GQA)
    return (summed, peak_score, totals)


def general_plan(
    prompt_states,
    prompt_lengths,
    prompt_owner,
    kv_weight,
    sampler_prompts,
    step_queries,
    step_kv,
    out_weight,
):
    states = prompt_states[0]
    own_pages = lax.psum_scatter(
        lax.dot_general(
            kv_weight, states, (((0,), (1,)), ((), ())), preferred_element_type=jnp.float32
        ).astype(jnp.bfloat16),
        "head",
        scatter_dimension=0,
        tiled=True,
    )
    step_count = step_queries.shape[0]
    row_total = step_queries.shape[1]
    prompt_count = sampler_prompts.shape[0]
    block_rows = row_total // prompt_count
    head_width = step_queries.shape[2]
    groups = own_pages.shape[0] // (2 * HD)
    owner_slots = jnp.take(prompt_owner, sampler_prompts)
    block_lengths = jnp.take(prompt_lengths, sampler_prompts)
    block_queries = [
        step_queries[:, position * block_rows : (position + 1) * block_rows].reshape(
            step_count * block_rows, head_width
        )
        for position in range(prompt_count)
    ]
    library = lax.all_gather(own_pages[None], "samp", axis=0, tiled=True)
    partials = []
    for position in range(prompt_count):
        page_block = lax.dynamic_index_in_dim(library, owner_slots[position], 0, keepdims=False)
        partials.append(
            prompt_partial(block_queries[position], page_block, block_lengths[position])
        )
    prompt_sum = jnp.concatenate(
        [entry[0].reshape(step_count, block_rows, groups, GQA, HD) for entry in partials], axis=1
    )
    prompt_peak = jnp.concatenate(
        [entry[1].reshape(step_count, block_rows, groups, GQA) for entry in partials], axis=1
    )
    prompt_total = jnp.concatenate(
        [entry[2].reshape(step_count, block_rows, groups, GQA) for entry in partials], axis=1
    )
    score_scale = 1.0 / math.sqrt(HD)
    query_all = step_queries.reshape(step_count, row_total, groups, GQA, HD)
    own_cache = step_kv.reshape(step_count, row_total, groups, 2, HD)
    near_scores = (
        jnp.einsum(
            "trgjd,urgd->trgju",
            query_all,
            own_cache[:, :, :, 0],
            preferred_element_type=jnp.float32,
        )
        * score_scale
    )
    causal = lax.broadcasted_iota(jnp.int32, near_scores.shape, 4) <= lax.broadcasted_iota(
        jnp.int32, near_scores.shape, 0
    )
    near_peak = jnp.max(jnp.where(causal, near_scores, masked_score), axis=4)
    near_weights = jnp.where(causal, jnp.exp(near_scores - near_peak[..., None]), 0.0)
    near_total = jnp.sum(near_weights, axis=4)
    near_sum = jnp.einsum(
        "trgju,urgd->trgjd",
        near_weights.astype(jnp.bfloat16),
        own_cache[:, :, :, 1],
        preferred_element_type=jnp.float32,
    )
    peak_all = jnp.maximum(prompt_peak, near_peak)
    far_factor = jnp.exp(prompt_peak - peak_all)
    near_factor = jnp.exp(near_peak - peak_all)
    numerator = prompt_sum * far_factor[..., None] + near_sum * near_factor[..., None]
    denominator = prompt_total * far_factor + near_total * near_factor
    attention = (numerator / denominator[..., None]).astype(jnp.bfloat16)
    attention = attention.reshape(step_count * row_total, groups * GQA * HD)
    terms = jnp.dot(
        attention,
        lax.all_gather(out_weight, "samp", axis=1, tiled=True),
        preferred_element_type=jnp.float32,
    )
    mixed = lax.psum_scatter(
        terms.astype(jnp.bfloat16), "head", scatter_dimension=1, tiled=True
    ).astype(jnp.float32)
    return mixed.astype(jnp.bfloat16).reshape(step_count, row_total, mixed.shape[1])


VMEM = 24 * 1024 * 1024
LARGE_VMEM = 60 * 1024 * 1024

CORE = [(0, 1), (1, 0), (2, 3), (3, 2)]
ACROSS_X = [(0, 2), (2, 0), (1, 3), (3, 1)]
INWARD = [(0, 1), (3, 2)]
MIDDLE = [(1, 2), (2, 1)]


def compiler_params(limit=VMEM):
    return pltpu.CompilerParams(vmem_limit_bytes=limit)


def small_cost():
    return pl.CostEstimate(flops=64, bytes_accessed=64, transcendentals=0)


def project(here, states, weight, masks, cuts):
    features, width = weight.shape[0], weight.shape[1] // 4
    parts = [(low, high - low) for low, high in zip(cuts[:-1], cuts[1:])]

    def body(here_ref, state_hbm, weight_hbm, *rest):
        outs, (state, blocks, state_sems, block_sems) = rest[: 2 * len(parts)], rest[2 * len(parts) :]
        fetches, blocks_in = [], []
        for side in range(2):
            place = here_ref[2] ^ masks[side]
            columns = pl.ds(pl.multiple_of(place * width, width), width)
            blocks_in.append(
                pltpu.make_async_copy(
                    weight_hbm.at[:, columns], blocks.at[side], block_sems.at[side]
                )
            )
        for at, (low, rows) in enumerate(parts):
            fetches.append(
                pltpu.make_async_copy(
                    state_hbm.at[low : low + rows], state.at[low : low + rows], state_sems.at[at]
                )
            )
        blocks_in[0].start()
        fetches[0].start()
        blocks_in[1].start()
        for fetch in fetches[1:]:
            fetch.start()
        for at, (low, rows) in enumerate(parts):
            fetches[at].wait()
            for side in range(2):
                if at == 0:
                    blocks_in[side].wait()
                outs[side * len(parts) + at][...] = jnp.dot(
                    state[low : low + rows], blocks[side], preferred_element_type=jnp.float32
                ).astype(jnp.bfloat16)

    in_hbm = pl.BlockSpec(memory_space=pltpu.HBM)
    in_vmem = pl.BlockSpec(memory_space=pltpu.VMEM)
    outs = pl.pallas_call(
        body,
        in_specs=[pl.BlockSpec(memory_space=pltpu.SMEM), in_hbm, in_hbm],
        out_specs=[in_vmem] * (2 * len(parts)),
        out_shape=[jax.ShapeDtypeStruct((rows, width), jnp.bfloat16) for _, rows in parts] * 2,
        scratch_shapes=[
            pltpu.VMEM(states.shape, jnp.bfloat16),
            pltpu.VMEM((2, features, width), jnp.bfloat16),
            pltpu.SemaphoreType.DMA((len(parts),)),
            pltpu.SemaphoreType.DMA((2,)),
        ],
        compiler_params=compiler_params(LARGE_VMEM),
        cost_estimate=small_cost(),
        name="project",
    )(here, states, weight)
    return outs[: len(parts)], outs[len(parts) :]


def attend(chosen, here, prompts, owners, lengths, queries, news, pages):
    news, new_start = news
    steps, rows, _ = queries.shape
    blocks = prompts.shape[0]
    block_rows = rows // blocks
    new_width = pages[0][0].shape[1]
    groups = new_width // (2 * HD)
    width = groups * GQA * HD
    tokens = sum(part.shape[0] for part in pages[0])
    count = chosen[1] - chosen[0]
    page_parts = [part for page in pages for part in page]
    tiles = 4
    chunk = tokens // tiles
    flat = steps * block_rows
    factor = math.log2(math.e) / math.sqrt(HD)

    def body(here_ref, prompts_ref, owners_ref, lengths_ref, query_hbm, new_hbm, *rest):
        page_refs, rest = rest[: len(page_parts)], rest[len(page_parts) :]
        out_ref, held, query_ref, new_ref, sems = rest
        plane = here_ref[1]

        def run(at, written, used, length):
            query = query_ref[at].reshape(flat, width)
            new = new_ref[at].reshape(flat, new_width)
            shape = (GQA * flat, flat)
            asker = lax.broadcasted_iota(jnp.int32, shape, 0) % flat
            holder = lax.broadcasted_iota(jnp.int32, shape, 1)
            near_ok = jnp.logical_and(asker % block_rows == holder % block_rows, holder <= asker)
            last = (GQA * flat, chunk)
            last_ok = lax.broadcasted_iota(jnp.int32, last, 1) < length - (used - chunk)
            for group in range(groups):
                key = slice(2 * group * HD, (2 * group + 1) * HD)
                value = slice((2 * group + 1) * HD, (2 * group + 2) * HD)
                asked = jnp.concatenate(
                    [
                        query[:, (group * GQA + head) * HD : (group * GQA + head + 1) * HD]
                        for head in range(GQA)
                    ],
                    axis=0,
                )

                def scores(keys):
                    return lax.dot_general(
                        asked, keys, (((1,), (1,)), ((), ())), preferred_element_type=jnp.float32
                    )

                parts = [
                    scores(held[at, tile * chunk : (tile + 1) * chunk, key])
                    for tile in range(used // chunk)
                ]
                parts[-1] = jnp.where(last_ok, parts[-1], masked_score)
                parts.append(jnp.where(near_ok, scores(new[:, key]), masked_score))
                peak = jnp.max(parts[0], axis=1, keepdims=True)
                for part in parts[1:]:
                    peak = jnp.maximum(peak, jnp.max(part, axis=1, keepdims=True))
                total, summed = 0.0, 0.0
                for tile, part in enumerate(parts):
                    weights = jnp.exp2((part - peak) * factor)
                    total = total + jnp.sum(weights, axis=1, keepdims=True)
                    values = (
                        held[at, tile * chunk : (tile + 1) * chunk, value]
                        if tile < len(parts) - 1
                        else new[:, value]
                    )
                    summed = summed + jnp.dot(
                        weights.astype(jnp.bfloat16), values, preferred_element_type=jnp.float32
                    )
                result = (summed / total).astype(jnp.bfloat16)
                for head in range(GQA):
                    column = (group * GQA + head) * HD
                    out_ref[:, written, column : column + HD] = result[
                        head * flat : (head + 1) * flat
                    ].reshape(steps, block_rows, HD)

        for block in range(*chosen):
            at = block - chosen[0]
            mine = slice(block * block_rows, (block + 1) * block_rows)
            pltpu.make_async_copy(
                query_hbm.at[:, mine, :width], query_ref.at[at], sems.at[0, at]
            ).start()
            pltpu.make_async_copy(
                new_hbm.at[:, mine, new_start : new_start + new_width], new_ref.at[at], sems.at[1, at]
            ).start()
            slot, passed = owners_ref[prompts_ref[block]], 0
            for page, place in zip(pages, (plane, plane ^ 1, 3 - plane, (3 - plane) ^ 1)):
                refs = page_refs[passed : passed + len(page)]
                passed += len(page)

                @pl.when(slot == place)
                def _():
                    low = 0
                    for ref in refs:
                        target = held.at[at, low : low + ref.shape[0]]
                        pltpu.make_async_copy(ref, target, sems.at[2, at]).start()
                        low += ref.shape[0]

        @pl.loop(0, count)
        def _(at):
            written = pl.ds(pl.multiple_of(at * block_rows, block_rows), block_rows)
            for kind, buffer in enumerate((query_ref, new_ref, held)):
                whole = buffer.at[at]
                pltpu.make_async_copy(whole, whole, sems.at[kind, at]).wait()
            length = lengths_ref[prompts_ref[chosen[0] + at]]
            for used in range(1, tiles + 1):
                enough = length > (used - 1) * chunk
                if used < tiles:
                    enough = jnp.logical_and(enough, length <= used * chunk)

                @pl.when(enough)
                def _():
                    run(at, written, used * chunk, length)

    in_vmem, in_smem, in_hbm = (
        pl.BlockSpec(memory_space=space) for space in (pltpu.VMEM, pltpu.SMEM, pltpu.HBM)
    )
    return pl.pallas_call(
        body,
        in_specs=[in_smem] * 4 + [in_hbm] * (2 + len(page_parts)),
        out_specs=in_vmem,
        out_shape=jax.ShapeDtypeStruct(
            (steps, count * block_rows, width), jnp.bfloat16
        ),
        scratch_shapes=[
            pltpu.VMEM((count, tokens, new_width), jnp.bfloat16),
            pltpu.VMEM((count, steps, block_rows, width), jnp.bfloat16),
            pltpu.VMEM((count, steps, block_rows, new_width), jnp.bfloat16),
            pltpu.SemaphoreType.DMA((3, count)),
        ],
        compiler_params=compiler_params(LARGE_VMEM),
        cost_estimate=small_cost(),
        name="attend",
    )(here, prompts, owners, lengths, queries, news, *page_parts)


def spread(here, blocks, own_weight, moved_weights):
    count, moved_count = len(blocks), len(moved_weights)
    steps, _, features = blocks[0].shape
    columns = own_weight.shape[1]
    tile = 256 if columns % 256 == 0 else columns
    ends = [0]
    for block in blocks:
        ends.append(ends[-1] + block.shape[1])
    places = [slice(low, high) for low, high in zip(ends[:-1], ends[1:])]

    def body(here_ref, *refs):
        row_refs, own_ref, refs = refs[:count], refs[count], refs[count + 1 :]
        moved_refs, refs = refs[:moved_count], refs[moved_count:]
        keep_ref, send_refs, taken_ref = refs[0], refs[1:-1], refs[-1]
        for ref, place in zip(row_refs, places):
            flat = slice(steps * place.start, steps * place.stop)
            taken_ref[flat] = ref[...].reshape(flat.stop - flat.start, features)
        taken = taken_ref[...]
        pieces = []
        for low, other, part in moved_weights:
            start = (here_ref[0] ^ other) * (features // 2) + low
            pieces.append(taken_ref[:, pl.ds(pl.multiple_of(start, 128), part.shape[0])])
        keeps_own = (here_ref[1] ^ here_ref[2]) % 2 == 0
        for column in range(0, columns, tile):
            part = slice(column, column + tile)
            own = jnp.dot(taken, own_ref[:, part], preferred_element_type=jnp.float32)
            moved = 0.0
            for piece, moved_ref in zip(pieces, moved_refs):
                moved = moved + jnp.dot(
                    piece, moved_ref[:, part], preferred_element_type=jnp.float32
                )
            keep = jnp.where(keeps_own, own, moved).astype(jnp.bfloat16)
            send = jnp.where(keeps_own, moved, own).astype(jnp.bfloat16)
            for place, send_ref in zip(places, send_refs):
                flat = slice(steps * place.start, steps * place.stop)
                shape = (steps, place.stop - place.start, tile)
                keep_ref[:, place, part] = keep[flat].reshape(shape)
                send_ref[:, :, part] = send[flat].reshape(shape)

    in_vmem = pl.BlockSpec(memory_space=pltpu.VMEM)
    out_rows = [ends[-1], *[block.shape[1] for block in blocks]]
    keep, *sends = pl.pallas_call(
        body,
        in_specs=[pl.BlockSpec(memory_space=pltpu.SMEM)] + [in_vmem] * (count + 1 + moved_count),
        out_specs=[in_vmem] * (1 + count),
        out_shape=[jax.ShapeDtypeStruct((steps, rows, columns), jnp.bfloat16) for rows in out_rows],
        scratch_shapes=[pltpu.VMEM((steps * ends[-1], features), jnp.bfloat16)],
        compiler_params=compiler_params(),
        cost_estimate=small_cost(),
        name="spread",
    )(here, *blocks, own_weight, *[part for _, _, part in moved_weights])
    return keep, sends


def run_small(body, name, here, operands, out_shape, outs=1, limit=VMEM, waits_for=()):
    in_vmem = pl.BlockSpec(memory_space=pltpu.VMEM)

    def whole(*refs):
        body(*refs[: 1 + len(operands)], *refs[1 + len(operands) + len(waits_for) :])

    return pl.pallas_call(
        whole,
        in_specs=[pl.BlockSpec(memory_space=pltpu.SMEM)]
        + [in_vmem] * len(operands)
        + [pl.BlockSpec(memory_space=pltpu.HBM)] * len(waits_for),
        out_specs=[in_vmem] * outs,
        out_shape=[jax.ShapeDtypeStruct(out_shape, jnp.bfloat16)] * outs,
        compiler_params=compiler_params(limit),
        cost_estimate=small_cost(),
        name=name,
    )(here, *operands, *waits_for)


def added(here, *parts, limit=VMEM):
    def body(_, *refs):
        total = refs[0][...].astype(jnp.float32)
        for ref in refs[1:-1]:
            total = total + ref[...].astype(jnp.float32)
        refs[-1][...] = total.astype(jnp.bfloat16)

    return run_small(body, "added", here, parts, parts[0].shape, limit=limit)[0]


def added_pieces(here, one, two, pieces, waits_for):
    steps, rows, columns = one.shape
    piece = rows // pieces

    def body(_, one_ref, two_ref, *outs):
        total = one_ref[...].astype(jnp.float32) + two_ref[...].astype(jnp.float32)
        total = total.astype(jnp.bfloat16)
        for at, out in enumerate(outs):
            out[...] = total[:, at * piece : (at + 1) * piece]

    shape = (steps, piece, columns)
    return run_small(body, "added_pieces", here, (one, two), shape, pieces, waits_for=waits_for)


def joined(here, ones, twos, waits_for):
    steps, piece, columns = ones[0].shape
    count = len(ones)

    def body(_, *refs):
        for at in range(count):
            total = refs[at][...].astype(jnp.float32) + refs[count + at][...].astype(jnp.float32)
            refs[-1][:, at * piece : (at + 1) * piece] = total.astype(jnp.bfloat16)

    shape = (steps, count * piece, columns)
    return run_small(body, "joined", here, (*ones, *twos), shape, waits_for=waits_for)[0]


def stacked(here, *parts, waits_for):
    rows = [part.shape[0] for part in parts]

    def body(_, *refs):
        for at, ref in enumerate(refs[:-1]):
            refs[-1][sum(rows[:at]) : sum(rows[: at + 1])] = ref[...]

    shape = (sum(rows), *parts[0].shape[1:])
    return run_small(body, "stacked", here, parts, shape, waits_for=waits_for)[0]


def added_half(here, mine, keep, sends, crossed=None):
    steps, rows, columns = keep.shape
    half, count = steps // 2, len(sends)
    ends = [sum(send.shape[1] for send in sends[:at]) for at in range(count + 1)]

    def body(here_ref, keep_ref, *refs):
        chip = here_ref[2] // 2
        taken = pl.ds((chip if mine else 1 - chip) * half, half)
        for at in range(count):
            place = slice(ends[at], ends[at + 1])
            total = keep_ref[taken, place].astype(jnp.float32) + refs[at][taken].astype(jnp.float32)
            if crossed is not None:
                total = total + refs[count][:, place].astype(jnp.float32)
            refs[-1][:, place] = total.astype(jnp.bfloat16)

    operands = (keep, *sends) if crossed is None else (keep, *sends, crossed)
    return run_small(body, "added_half", here, operands, (half, rows, columns))[0]


def added_halves(here, keep, sends, crossed):
    steps, rows, columns = keep.shape
    half, piece = steps // 2, rows // 2

    def body(here_ref, keep_ref, far_ref, end_ref, crossed_ref, first_ref, second_ref):
        chip = here_ref[2] // 2
        taken = pl.ds(chip * half, half)
        total = keep_ref[taken].astype(jnp.float32) + crossed_ref[...].astype(jnp.float32)
        far = (total[:, :piece] + far_ref[taken].astype(jnp.float32)).astype(jnp.bfloat16)
        end = (total[:, piece:] + end_ref[taken].astype(jnp.float32)).astype(jnp.bfloat16)
        at_home = here_ref[1] // 2 == chip

        @pl.when(at_home)
        def _():
            first_ref[...] = far
            second_ref[...] = end

        @pl.when(jnp.logical_not(at_home))
        def _():
            first_ref[...] = end
            second_ref[...] = far

    shape = (half, piece, columns)
    return run_small(body, "added_halves", here, (keep, *sends, crossed), shape, 2)


def after(value, *others):
    return lax.optimization_barrier((value, *others))[0]


def home_pairs(target, turned):
    pairs = []
    for source in (1, 2):
        side = source // 2
        chip = 1 - side if turned else side
        for at in range(2):
            pairs.append((source * 4 + 2 * chip + at, target(source) * 4 + 2 * side + at))
    return pairs


def sent_home(value, *pairs):
    return lax.ppermute(value, ("samp", "head"), [pair for part in pairs for pair in part])


def across_home(value):
    pairs = [
        (source * 4 + 2 * (1 - source // 2) + at, source * 4 + 2 * (source // 2) + at)
        for source in (1, 2)
        for at in range(2)
    ]
    return lax.ppermute(value, ("samp", "head"), pairs)


def inward_plan(
    prompt_states,
    prompt_lengths,
    prompt_owner,
    kv_weight,
    sampler_prompts,
    step_queries,
    step_kv,
    out_weight,
):
    group, plane, head = (lax.axis_index(name) for name in ("groups", "samp", "head"))
    chip = head // 2
    here = jnp.stack([group, plane, head]).astype(jnp.int32)

    def on_samp(value, pairs):
        return lax.ppermute(value, "samp", pairs)

    def on_head(value, pairs):
        return lax.ppermute(value, "head", pairs)

    def hopped(*values):
        token = here
        for value in values:
            token = on_head(after(token, *value), CORE)
        return token

    def beside(value, *others):
        return on_head(after(value, *others), CORE)

    states = prompt_states[0]
    tokens = states.shape[0]
    cuts = [0, tokens * 7 // 16, tokens]
    sent, kept = project(here, states, kv_weight, (3, 2), cuts)

    half = out_weight.shape[0] // 2
    weight_cuts = [0, half * 2 // 5, half]

    def weight_part(at, *others):
        low, size = weight_cuts[at], weight_cuts[at + 1] - weight_cuts[at]
        return lax.dynamic_slice_in_dim(after(out_weight, *others), group * half + low, size, 0)

    def swapped(part):
        return lax.ppermute(part, "groups", [(0, 1), (1, 0)])

    weight_0 = on_samp(weight_part(0, sent[0]), INWARD)
    leaving_first = added(here, kept[0], on_head(sent[0], CORE), limit=LARGE_VMEM)
    leaving_second = added(here, kept[1], after(on_head(sent[1], CORE), leaving_first), limit=LARGE_VMEM)
    crossed_first = on_head(leaving_first, ACROSS_X)
    crossed_second = on_head(leaving_second, ACROSS_X)
    sent, kept = project(
        here, after(states, leaving_first, leaving_second), kv_weight, (1, 0), cuts
    )
    sent = [on_head(value, CORE) for value in sent]
    first = added(hopped((crossed_first,)), kept[0], sent[0], crossed_first, limit=LARGE_VMEM)
    end_first = on_samp(after(first, weight_0), INWARD)
    far_first = on_samp(first, MIDDLE)
    second = added(hopped((crossed_second,)), kept[1], sent[1], crossed_second, limit=LARGE_VMEM)
    end_second = on_samp(second, INWARD)
    far_second = on_samp(second, MIDDLE)
    end_page = stacked(
        here, end_first, end_second, waits_for=(beside(leaving_first, far_first, end_first),)
    )
    moved_0 = swapped(weight_0)
    far_end_page = on_samp(after(end_page, far_second), MIDDLE)
    pages = ((first, second), (end_page,), (far_first, far_second), (far_end_page,))
    end_prompts = on_samp(after(sampler_prompts, second), INWARD)
    weight_1 = on_samp(after(weight_part(1, first), end_second, end_prompts), INWARD)
    asked = jnp.concatenate([after(step_queries, first), step_kv], axis=2)
    end_asked = on_samp(after(asked, weight_1), INWARD)
    parts = ((weight_0, moved_0), (weight_1, swapped(weight_1)))
    moved_weights = [
        (low, side, part[side]) for side in range(2) for low, part in zip(weight_cuts, parts)
    ]

    def attended(place, chosen, prompts, queries, news):
        rows = attend(
            chosen, place, prompts, prompt_owner, prompt_lengths, queries, news, pages
        )
        return rows, on_samp(rows, MIDDLE)

    def spread_out(*blocks, place=here):
        keep, sends = spread(place, blocks, out_weight, moved_weights)
        return keep, [on_head(send, CORE) for send in sends]

    blocks = sampler_prompts.shape[0]
    own_rows, far_own_rows = attended(
        here, (0, blocks), sampler_prompts, after(step_queries, moved_0), (step_kv, 0)
    )
    end_rows, far_end_rows = attended(
        here,
        (0, blocks),
        end_prompts,
        after(end_asked, own_rows),
        (end_asked, step_queries.shape[2]),
    )
    both_keep, both_arrived = spread_out(far_own_rows, end_rows)
    own_keep, own_arrived = spread_out(after(own_rows, both_keep))
    place = hopped((far_end_rows,), (far_end_rows,))
    both_leaving = added_half(place, False, both_keep, both_arrived)
    both_crossed = on_head(both_leaving, ACROSS_X)
    beyond_keep, beyond_arrived = spread_out(after(far_end_rows, own_keep, both_leaving))
    beyond_leaving = added_half(here, False, beyond_keep, beyond_arrived)
    beyond_crossed = on_head(beyond_leaving, ACROSS_X)
    own_chip = added_pieces(
        here,
        own_keep,
        after(own_arrived[0], beyond_leaving),
        2,
        waits_for=(beside(own_rows, both_crossed),),
    )
    own_crossed = [
        across_home(after(part, earlier))
        for part, earlier in zip(own_chip, (both_crossed, beyond_crossed))
    ]
    first_sum, second_sum = added_halves(here, both_keep, both_arrived, both_crossed)

    def far(at):
        return 3 - at

    def end(at):
        return at ^ 1

    def beyond(at):
        return (3 - at) ^ 1

    first_home = sent_home(first_sum, home_pairs(far, False), home_pairs(end, True))
    second_home = sent_home(second_sum, home_pairs(far, True), home_pairs(end, False))
    beyond_sum = added_half(
        here, True, beyond_keep, beyond_arrived, beyond_crossed
    )
    beyond_home = [sent_home(beyond_sum, home_pairs(beyond, turned)) for turned in (False, True)]
    own_home = joined(
        here, own_chip, own_crossed, waits_for=(beside(own_keep, own_crossed[0]),)
    )

    is_middle = jnp.logical_or(plane == 1, plane == 2)
    near_side = chip == plane // 2
    straight = jnp.where(is_middle, first_home, jnp.where(near_side, second_home, beyond_home[0]))
    turned = jnp.where(is_middle, second_home, jnp.where(near_side, first_home, beyond_home[1]))
    return jnp.where(
        jnp.logical_and(is_middle, near_side),
        own_home,
        jnp.where(
            chip == 0,
            jnp.concatenate([straight, turned], axis=0),
            jnp.concatenate([turned, straight], axis=0),
        ),
    )


def solution(mesh):
    line, width = mesh.shape["samp"], mesh.shape["head"]
    paired = line == 4 and width == 4 and mesh.shape["groups"] == 2
    on_device = inward_plan if paired else general_plan

    placed = (
        P(("groups", "samp"), None, "head"),
        P("groups"),
        P("groups"),
        P("head", None),
        P(("groups", "samp")),
        P(None, ("groups", "samp"), "head"),
        P(None, ("groups", "samp"), "head"),
        P("head", "samp"),
    )
    return jax.shard_map(
        on_device,
        mesh=mesh,
        in_specs=placed,
        out_specs=P(None, ("groups", "samp"), "head"),
        check_vma=False,
    )
```

```python
import math

import jax
import jax.numpy as jnp
from jax import lax
from jax.experimental import pallas as pl
from jax.experimental.pallas import tpu as pltpu
from jax.sharding import PartitionSpec as P

HD = 128
GQA = 5


masked_score = -1e30


def prompt_partial(queries, page_block, length):
    row_count = queries.shape[0]
    groups = page_block.shape[0] // (2 * HD)
    score_scale = 1.0 / math.sqrt(HD)
    query_heads = queries.reshape(row_count, groups, GQA, HD)
    page_heads = page_block.reshape(groups, 2, HD, page_block.shape[1])
    scores = (
        jnp.einsum(
            "rgjd,gdl->grjl", query_heads, page_heads[:, 0], preferred_element_type=jnp.float32
        )
        * score_scale
    )
    usable = lax.broadcasted_iota(jnp.int32, scores.shape, 3) < length
    peak_score = jnp.max(jnp.where(usable, scores, masked_score), axis=3)
    weights = jnp.where(usable, jnp.exp(scores - peak_score[..., None]), 0.0)
    totals = jnp.sum(weights, axis=3)
    summed = jnp.einsum(
        "grjl,gdl->grjd",
        weights.astype(jnp.bfloat16),
        page_heads[:, 1],
        preferred_element_type=jnp.float32,
    )
    summed = jnp.transpose(summed, (1, 0, 2, 3)).reshape(row_count, groups * GQA * HD)
    peak_score = jnp.transpose(peak_score, (1, 0, 2)).reshape(row_count, groups * GQA)
    totals = jnp.transpose(totals, (1, 0, 2)).reshape(row_count, groups * GQA)
    return (summed, peak_score, totals)


def general_plan(
    prompt_states,
    prompt_lengths,
    prompt_owner,
    kv_weight,
    sampler_prompts,
    step_queries,
    step_kv,
    out_weight,
):
    states = prompt_states[0]
    own_pages = lax.psum_scatter(
        lax.dot_general(
            kv_weight, states, (((0,), (1,)), ((), ())), preferred_element_type=jnp.float32
        ).astype(jnp.bfloat16),
        "head",
        scatter_dimension=0,
        tiled=True,
    )
    step_count = step_queries.shape[0]
    row_total = step_queries.shape[1]
    prompt_count = sampler_prompts.shape[0]
    block_rows = row_total // prompt_count
    head_width = step_queries.shape[2]
    groups = own_pages.shape[0] // (2 * HD)
    owner_slots = jnp.take(prompt_owner, sampler_prompts)
    block_lengths = jnp.take(prompt_lengths, sampler_prompts)
    block_queries = [
        step_queries[:, position * block_rows : (position + 1) * block_rows].reshape(
            step_count * block_rows, head_width
        )
        for position in range(prompt_count)
    ]
    library = lax.all_gather(own_pages[None], "samp", axis=0, tiled=True)
    partials = []
    for position in range(prompt_count):
        page_block = lax.dynamic_index_in_dim(library, owner_slots[position], 0, keepdims=False)
        partials.append(
            prompt_partial(block_queries[position], page_block, block_lengths[position])
        )
    prompt_sum = jnp.concatenate(
        [entry[0].reshape(step_count, block_rows, groups, GQA, HD) for entry in partials], axis=1
    )
    prompt_peak = jnp.concatenate(
        [entry[1].reshape(step_count, block_rows, groups, GQA) for entry in partials], axis=1
    )
    prompt_total = jnp.concatenate(
        [entry[2].reshape(step_count, block_rows, groups, GQA) for entry in partials], axis=1
    )
    score_scale = 1.0 / math.sqrt(HD)
    query_all = step_queries.reshape(step_count, row_total, groups, GQA, HD)
    own_cache = step_kv.reshape(step_count, row_total, groups, 2, HD)
    near_scores = (
        jnp.einsum(
            "trgjd,urgd->trgju",
            query_all,
            own_cache[:, :, :, 0],
            preferred_element_type=jnp.float32,
        )
        * score_scale
    )
    causal = lax.broadcasted_iota(jnp.int32, near_scores.shape, 4) <= lax.broadcasted_iota(
        jnp.int32, near_scores.shape, 0
    )
    near_peak = jnp.max(jnp.where(causal, near_scores, masked_score), axis=4)
    near_weights = jnp.where(causal, jnp.exp(near_scores - near_peak[..., None]), 0.0)
    near_total = jnp.sum(near_weights, axis=4)
    near_sum = jnp.einsum(
        "trgju,urgd->trgjd",
        near_weights.astype(jnp.bfloat16),
        own_cache[:, :, :, 1],
        preferred_element_type=jnp.float32,
    )
    peak_all = jnp.maximum(prompt_peak, near_peak)
    far_factor = jnp.exp(prompt_peak - peak_all)
    near_factor = jnp.exp(near_peak - peak_all)
    numerator = prompt_sum * far_factor[..., None] + near_sum * near_factor[..., None]
    denominator = prompt_total * far_factor + near_total * near_factor
    attention = (numerator / denominator[..., None]).astype(jnp.bfloat16)
    attention = attention.reshape(step_count * row_total, groups * GQA * HD)
    terms = jnp.dot(
        attention,
        lax.all_gather(out_weight, "samp", axis=1, tiled=True),
        preferred_element_type=jnp.float32,
    )
    mixed = lax.psum_scatter(
        terms.astype(jnp.bfloat16), "head", scatter_dimension=1, tiled=True
    ).astype(jnp.float32)
    return mixed.astype(jnp.bfloat16).reshape(step_count, row_total, mixed.shape[1])


VMEM = 24 * 1024 * 1024
LARGE_VMEM = 60 * 1024 * 1024

CORE = [(0, 1), (1, 0), (2, 3), (3, 2)]
ACROSS_X = [(0, 2), (2, 0), (1, 3), (3, 1)]
INWARD = [(0, 1), (3, 2)]
MIDDLE = [(1, 2), (2, 1)]


def compiler_params(limit=VMEM):
    return pltpu.CompilerParams(vmem_limit_bytes=limit)


def small_cost():
    return pl.CostEstimate(flops=64, bytes_accessed=64, transcendentals=0)


def project(here, states, weight, masks, cuts):
    features, width = weight.shape[0], weight.shape[1] // 4
    parts = [(low, high - low) for low, high in zip(cuts[:-1], cuts[1:])]

    def body(here_ref, state_hbm, weight_hbm, *rest):
        outs, (state, blocks, state_sems, block_sems) = rest[: 2 * len(parts)], rest[2 * len(parts) :]
        fetches, blocks_in = [], []
        for side in range(2):
            place = here_ref[2] ^ masks[side]
            columns = pl.ds(pl.multiple_of(place * width, width), width)
            blocks_in.append(
                pltpu.make_async_copy(
                    weight_hbm.at[:, columns], blocks.at[side], block_sems.at[side]
                )
            )
        for at, (low, rows) in enumerate(parts):
            fetches.append(
                pltpu.make_async_copy(
                    state_hbm.at[low : low + rows], state.at[low : low + rows], state_sems.at[at]
                )
            )
        blocks_in[0].start()
        fetches[0].start()
        blocks_in[1].start()
        for fetch in fetches[1:]:
            fetch.start()
        for at, (low, rows) in enumerate(parts):
            fetches[at].wait()
            for side in range(2):
                if at == 0:
                    blocks_in[side].wait()
                outs[side * len(parts) + at][...] = jnp.dot(
                    state[low : low + rows], blocks[side], preferred_element_type=jnp.float32
                ).astype(jnp.bfloat16)

    in_hbm = pl.BlockSpec(memory_space=pltpu.HBM)
    in_vmem = pl.BlockSpec(memory_space=pltpu.VMEM)
    outs = pl.pallas_call(
        body,
        in_specs=[pl.BlockSpec(memory_space=pltpu.SMEM), in_hbm, in_hbm],
        out_specs=[in_vmem] * (2 * len(parts)),
        out_shape=[jax.ShapeDtypeStruct((rows, width), jnp.bfloat16) for _, rows in parts] * 2,
        scratch_shapes=[
            pltpu.VMEM(states.shape, jnp.bfloat16),
            pltpu.VMEM((2, features, width), jnp.bfloat16),
            pltpu.SemaphoreType.DMA((len(parts),)),
            pltpu.SemaphoreType.DMA((2,)),
        ],
        compiler_params=compiler_params(LARGE_VMEM),
        cost_estimate=small_cost(),
        name="project",
    )(here, states, weight)
    return outs[: len(parts)], outs[len(parts) :]


def attend(chosen, here, prompts, owners, lengths, queries, news, pages):
    news, new_start = news
    steps, rows, _ = queries.shape
    blocks = prompts.shape[0]
    block_rows = rows // blocks
    new_width = pages[0][0].shape[1]
    groups = new_width // (2 * HD)
    width = groups * GQA * HD
    tokens = sum(part.shape[0] for part in pages[0])
    count = chosen[1] - chosen[0]
    page_parts = [part for page in pages for part in page]
    tiles = 4
    chunk = tokens // tiles
    flat = steps * block_rows
    factor = math.log2(math.e) / math.sqrt(HD)

    def body(here_ref, prompts_ref, owners_ref, lengths_ref, query_hbm, new_hbm, *rest):
        page_refs, rest = rest[: len(page_parts)], rest[len(page_parts) :]
        out_ref, held, query_ref, new_ref, sems = rest
        plane = here_ref[1]

        def run(at, written, used, length):
            query = query_ref[at].reshape(flat, width)
            new = new_ref[at].reshape(flat, new_width)
            shape = (GQA * flat, flat)
            asker = lax.broadcasted_iota(jnp.int32, shape, 0) % flat
            holder = lax.broadcasted_iota(jnp.int32, shape, 1)
            near_ok = jnp.logical_and(asker % block_rows == holder % block_rows, holder <= asker)
            last = (GQA * flat, chunk)
            last_ok = lax.broadcasted_iota(jnp.int32, last, 1) < length - (used - chunk)
            for group in range(groups):
                key = slice(2 * group * HD, (2 * group + 1) * HD)
                value = slice((2 * group + 1) * HD, (2 * group + 2) * HD)
                asked = jnp.concatenate(
                    [
                        query[:, (group * GQA + head) * HD : (group * GQA + head + 1) * HD]
                        for head in range(GQA)
                    ],
                    axis=0,
                )

                def scores(keys):
                    return lax.dot_general(
                        asked, keys, (((1,), (1,)), ((), ())), preferred_element_type=jnp.float32
                    )

                parts = [
                    scores(held[at, tile * chunk : (tile + 1) * chunk, key])
                    for tile in range(used // chunk)
                ]
                parts[-1] = jnp.where(last_ok, parts[-1], masked_score)
                parts.append(jnp.where(near_ok, scores(new[:, key]), masked_score))
                peak = jnp.max(parts[0], axis=1, keepdims=True)
                for part in parts[1:]:
                    peak = jnp.maximum(peak, jnp.max(part, axis=1, keepdims=True))
                total, summed = 0.0, 0.0
                for tile, part in enumerate(parts):
                    weights = jnp.exp2((part - peak) * factor)
                    total = total + jnp.sum(weights, axis=1, keepdims=True)
                    values = (
                        held[at, tile * chunk : (tile + 1) * chunk, value]
                        if tile < len(parts) - 1
                        else new[:, value]
                    )
                    summed = summed + jnp.dot(
                        weights.astype(jnp.bfloat16), values, preferred_element_type=jnp.float32
                    )
                result = (summed / total).astype(jnp.bfloat16)
                for head in range(GQA):
                    column = (group * GQA + head) * HD
                    out_ref[:, written, column : column + HD] = result[
                        head * flat : (head + 1) * flat
                    ].reshape(steps, block_rows, HD)

        for block in range(*chosen):
            at = block - chosen[0]
            mine = slice(block * block_rows, (block + 1) * block_rows)
            pltpu.make_async_copy(
                query_hbm.at[:, mine, :width], query_ref.at[at], sems.at[0, at]
            ).start()
            pltpu.make_async_copy(
                new_hbm.at[:, mine, new_start : new_start + new_width], new_ref.at[at], sems.at[1, at]
            ).start()
            slot, passed = owners_ref[prompts_ref[block]], 0
            for page, place in zip(pages, (plane, plane ^ 1, 3 - plane, (3 - plane) ^ 1)):
                refs = page_refs[passed : passed + len(page)]
                passed += len(page)

                @pl.when(slot == place)
                def _():
                    low = 0
                    for ref in refs:
                        target = held.at[at, low : low + ref.shape[0]]
                        pltpu.make_async_copy(ref, target, sems.at[2, at]).start()
                        low += ref.shape[0]

        @pl.loop(0, count)
        def _(at):
            written = pl.ds(pl.multiple_of(at * block_rows, block_rows), block_rows)
            for kind, buffer in enumerate((query_ref, new_ref, held)):
                whole = buffer.at[at]
                pltpu.make_async_copy(whole, whole, sems.at[kind, at]).wait()
            length = lengths_ref[prompts_ref[chosen[0] + at]]
            for used in range(1, tiles + 1):
                enough = length > (used - 1) * chunk
                if used < tiles:
                    enough = jnp.logical_and(enough, length <= used * chunk)

                @pl.when(enough)
                def _():
                    run(at, written, used * chunk, length)

    in_vmem, in_smem, in_hbm = (
        pl.BlockSpec(memory_space=space) for space in (pltpu.VMEM, pltpu.SMEM, pltpu.HBM)
    )
    return pl.pallas_call(
        body,
        in_specs=[in_smem] * 4 + [in_hbm] * (2 + len(page_parts)),
        out_specs=in_vmem,
        out_shape=jax.ShapeDtypeStruct(
            (steps, count * block_rows, width), jnp.bfloat16
        ),
        scratch_shapes=[
            pltpu.VMEM((count, tokens, new_width), jnp.bfloat16),
            pltpu.VMEM((count, steps, block_rows, width), jnp.bfloat16),
            pltpu.VMEM((count, steps, block_rows, new_width), jnp.bfloat16),
            pltpu.SemaphoreType.DMA((3, count)),
        ],
        compiler_params=compiler_params(40 * 1024 * 1024),
        cost_estimate=small_cost(),
        name="attend",
    )(here, prompts, owners, lengths, queries, news, *page_parts)


def spread(here, blocks, own_weight, moved_weights, waits_for):
    count, moved_count = len(blocks), len(moved_weights)
    steps, _, features = blocks[0].shape
    columns = own_weight.shape[1]
    tile = 256 if columns % 256 == 0 else columns
    ends = [0]
    for block in blocks:
        ends.append(ends[-1] + block.shape[1])
    places = [slice(low, high) for low, high in zip(ends[:-1], ends[1:])]

    def body(here_ref, *refs):
        row_refs, own_ref, refs = refs[:count], refs[count], refs[count + 1 :]
        moved_refs, refs = refs[:moved_count], refs[moved_count + len(waits_for) :]
        keep_ref, send_refs, taken_ref = refs[0], refs[1:-1], refs[-1]
        for ref, place in zip(row_refs, places):
            flat = slice(steps * place.start, steps * place.stop)
            taken_ref[flat] = ref[...].reshape(flat.stop - flat.start, features)
        taken = taken_ref[...]
        pieces = []
        for low, other, part in moved_weights:
            start = (here_ref[0] ^ other) * (features // 2) + low
            pieces.append(taken_ref[:, pl.ds(pl.multiple_of(start, 128), part.shape[0])])
        keeps_own = (here_ref[1] ^ here_ref[2]) % 2 == 0
        for column in range(0, columns, tile):
            part = slice(column, column + tile)
            own = jnp.dot(taken, own_ref[:, part], preferred_element_type=jnp.float32)
            moved = 0.0
            for piece, moved_ref in zip(pieces, moved_refs):
                moved = moved + jnp.dot(
                    piece, moved_ref[:, part], preferred_element_type=jnp.float32
                )
            keep = jnp.where(keeps_own, own, moved).astype(jnp.bfloat16)
            send = jnp.where(keeps_own, moved, own).astype(jnp.bfloat16)
            for place, send_ref in zip(places, send_refs):
                flat = slice(steps * place.start, steps * place.stop)
                shape = (steps, place.stop - place.start, tile)
                keep_ref[:, place, part] = keep[flat].reshape(shape)
                send_ref[:, :, part] = send[flat].reshape(shape)

    in_vmem = pl.BlockSpec(memory_space=pltpu.VMEM)
    out_rows = [ends[-1], *[block.shape[1] for block in blocks]]
    keep, *sends = pl.pallas_call(
        body,
        in_specs=[pl.BlockSpec(memory_space=pltpu.SMEM)] + [in_vmem] * (count + 1 + moved_count)
        + [pl.BlockSpec(memory_space=pltpu.HBM)] * len(waits_for),
        out_specs=[in_vmem] * (1 + count),
        out_shape=[jax.ShapeDtypeStruct((steps, rows, columns), jnp.bfloat16) for rows in out_rows],
        scratch_shapes=[pltpu.VMEM((steps * ends[-1], features), jnp.bfloat16)],
        compiler_params=compiler_params(),
        cost_estimate=small_cost(),
        name="spread",
    )(here, *blocks, own_weight, *[part for _, _, part in moved_weights], *waits_for)
    return keep, sends


def run_small(body, name, here, operands, out_shape, outs=1, limit=VMEM, waits_for=()):
    in_vmem = pl.BlockSpec(memory_space=pltpu.VMEM)

    def whole(*refs):
        body(*refs[: 1 + len(operands)], *refs[1 + len(operands) + len(waits_for) :])

    return pl.pallas_call(
        whole,
        in_specs=[pl.BlockSpec(memory_space=pltpu.SMEM)]
        + [in_vmem] * len(operands)
        + [pl.BlockSpec(memory_space=pltpu.HBM)] * len(waits_for),
        out_specs=[in_vmem] * outs,
        out_shape=[jax.ShapeDtypeStruct(out_shape, jnp.bfloat16)] * outs,
        compiler_params=compiler_params(limit),
        cost_estimate=small_cost(),
        name=name,
    )(here, *operands, *waits_for)


def added(here, *parts, limit=VMEM):
    def body(_, *refs):
        total = refs[0][...].astype(jnp.float32)
        for ref in refs[1:-1]:
            total = total + ref[...].astype(jnp.float32)
        refs[-1][...] = total.astype(jnp.bfloat16)

    return run_small(body, "added", here, parts, parts[0].shape, limit=limit)[0]


def added_pieces(here, one, two, pieces, waits_for):
    steps, rows, columns = one.shape
    piece = rows // pieces

    def body(_, one_ref, two_ref, *outs):
        total = one_ref[...].astype(jnp.float32) + two_ref[...].astype(jnp.float32)
        total = total.astype(jnp.bfloat16)
        for at, out in enumerate(outs):
            out[...] = total[:, at * piece : (at + 1) * piece]

    shape = (steps, piece, columns)
    return run_small(body, "added_pieces", here, (one, two), shape, pieces, waits_for=waits_for)


def joined(here, ones, twos, waits_for):
    steps, piece, columns = ones[0].shape
    count = len(ones)

    def body(_, *refs):
        for at in range(count):
            total = refs[at][...].astype(jnp.float32) + refs[count + at][...].astype(jnp.float32)
            refs[-1][:, at * piece : (at + 1) * piece] = total.astype(jnp.bfloat16)

    shape = (steps, count * piece, columns)
    return run_small(body, "joined", here, (*ones, *twos), shape, waits_for=waits_for)[0]


def stacked(here, *parts, waits_for):
    rows = [part.shape[0] for part in parts]

    def body(_, *refs):
        for at, ref in enumerate(refs[:-1]):
            refs[-1][sum(rows[:at]) : sum(rows[: at + 1])] = ref[...]

    shape = (sum(rows), *parts[0].shape[1:])
    return run_small(body, "stacked", here, parts, shape, waits_for=waits_for)[0]


def added_half(here, mine, keep, sends, crossed=None):
    steps, rows, columns = keep.shape
    half, count = steps // 2, len(sends)
    ends = [sum(send.shape[1] for send in sends[:at]) for at in range(count + 1)]

    def body(here_ref, keep_ref, *refs):
        chip = here_ref[2] // 2
        taken = pl.ds((chip if mine else 1 - chip) * half, half)
        for at in range(count):
            place = slice(ends[at], ends[at + 1])
            total = keep_ref[taken, place].astype(jnp.float32) + refs[at][taken].astype(jnp.float32)
            if crossed is not None:
                total = total + refs[count][:, place].astype(jnp.float32)
            refs[-1][:, place] = total.astype(jnp.bfloat16)

    operands = (keep, *sends) if crossed is None else (keep, *sends, crossed)
    return run_small(body, "added_half", here, operands, (half, rows, columns))[0]


def added_halves(here, keep, sends, crossed):
    steps, rows, columns = keep.shape
    half, piece = steps // 2, rows // 2

    def body(here_ref, keep_ref, far_ref, end_ref, crossed_ref, first_ref, second_ref):
        chip = here_ref[2] // 2
        taken = pl.ds(chip * half, half)
        total = keep_ref[taken].astype(jnp.float32) + crossed_ref[...].astype(jnp.float32)
        far = (total[:, :piece] + far_ref[taken].astype(jnp.float32)).astype(jnp.bfloat16)
        end = (total[:, piece:] + end_ref[taken].astype(jnp.float32)).astype(jnp.bfloat16)
        at_home = here_ref[1] // 2 == chip

        @pl.when(at_home)
        def _():
            first_ref[...] = far
            second_ref[...] = end

        @pl.when(jnp.logical_not(at_home))
        def _():
            first_ref[...] = end
            second_ref[...] = far

    shape = (half, piece, columns)
    return run_small(body, "added_halves", here, (keep, *sends, crossed), shape, 2)


def after(value, *others):
    return lax.optimization_barrier((value, *others))[0]


def home_pairs(target, turned):
    pairs = []
    for source in (1, 2):
        side = source // 2
        chip = 1 - side if turned else side
        for at in range(2):
            pairs.append((source * 4 + 2 * chip + at, target(source) * 4 + 2 * side + at))
    return pairs


def sent_home(value, *pairs):
    return lax.ppermute(value, ("samp", "head"), [pair for part in pairs for pair in part])


def across_home(value):
    pairs = [
        (source * 4 + 2 * (1 - source // 2) + at, source * 4 + 2 * (source // 2) + at)
        for source in (1, 2)
        for at in range(2)
    ]
    return lax.ppermute(value, ("samp", "head"), pairs)


def inward_plan(
    prompt_states,
    prompt_lengths,
    prompt_owner,
    kv_weight,
    sampler_prompts,
    step_queries,
    step_kv,
    out_weight,
):
    group, plane, head = (lax.axis_index(name) for name in ("groups", "samp", "head"))
    chip = head // 2
    here = jnp.stack([group, plane, head]).astype(jnp.int32)

    def on_samp(value, pairs):
        return lax.ppermute(value, "samp", pairs)

    def on_head(value, pairs):
        return lax.ppermute(value, "head", pairs)

    def hopped(*values):
        token = here
        for value in values:
            token = on_head(after(token, *value), CORE)
        return token

    def beside(value, *others):
        return on_head(after(value, *others), CORE)

    states = prompt_states[0]
    tokens = states.shape[0]
    cuts = [0, tokens * 7 // 16, tokens]
    sent, kept = project(here, states, kv_weight, (3, 2), cuts)

    half = out_weight.shape[0] // 2
    weight_cuts = [0, half * 2 // 5, half]

    def weight_part(at, *others):
        low, size = weight_cuts[at], weight_cuts[at + 1] - weight_cuts[at]
        return lax.dynamic_slice_in_dim(after(out_weight, *others), group * half + low, size, 0)

    def swapped(part):
        return lax.ppermute(part, "groups", [(0, 1), (1, 0)])

    weight_0 = on_samp(weight_part(0, sent[0]), INWARD)
    leaving_first = added(here, kept[0], on_head(sent[0], CORE), limit=LARGE_VMEM)
    leaving_second = added(here, kept[1], after(on_head(sent[1], CORE), leaving_first), limit=LARGE_VMEM)
    crossed_first = on_head(leaving_first, ACROSS_X)
    crossed_second = on_head(leaving_second, ACROSS_X)
    sent, kept = project(
        here, after(states, leaving_first, leaving_second), kv_weight, (1, 0), cuts
    )
    sent = [on_head(value, CORE) for value in sent]
    first = added(hopped((crossed_first,)), kept[0], sent[0], crossed_first, limit=LARGE_VMEM)
    end_first = on_samp(after(first, weight_0), INWARD)
    far_first = on_samp(first, MIDDLE)
    second = added(hopped((crossed_second,)), kept[1], sent[1], crossed_second, limit=LARGE_VMEM)
    end_second = on_samp(second, INWARD)
    far_second = on_samp(second, MIDDLE)
    end_page = stacked(
        here, end_first, end_second, waits_for=(beside(leaving_first, far_first, end_first),)
    )
    moved_0 = swapped(weight_0)
    far_end_page = on_samp(after(end_page, far_second), MIDDLE)
    pages = ((first, second), (end_page,), (far_first, far_second), (far_end_page,))
    end_prompts = on_samp(after(sampler_prompts, second), INWARD)
    weight_1 = on_samp(after(weight_part(1, first), end_second, end_prompts), INWARD)
    asked = jnp.concatenate([after(step_queries, first), step_kv], axis=2)
    end_asked = on_samp(after(asked, weight_1), INWARD)
    parts = ((weight_0, moved_0), (weight_1, swapped(weight_1)))
    moved_weights = [
        (low, side, part[side]) for side in range(2) for low, part in zip(weight_cuts, parts)
    ]

    def attended(place, chosen, prompts, queries, news):
        rows = attend(
            chosen, place, prompts, prompt_owner, prompt_lengths, queries, news, pages
        )
        return rows, on_samp(rows, MIDDLE)

    def spread_out(*blocks, waits_for=()):
        keep, sends = spread(here, blocks, out_weight, moved_weights, waits_for)
        return keep, [on_head(send, CORE) for send in sends]

    blocks = sampler_prompts.shape[0]
    own_rows, far_own_rows = attended(
        here, (0, blocks), sampler_prompts, after(step_queries, moved_0), (step_kv, 0)
    )
    end_rows, far_end_rows = attended(
        here,
        (0, blocks),
        end_prompts,
        after(end_asked, own_rows),
        (end_asked, step_queries.shape[2]),
    )
    both_keep, both_arrived = spread_out(far_own_rows, end_rows)
    own_keep, own_arrived = spread_out(after(own_rows, both_keep))
    both_leaving = added_half(here, False, both_keep, both_arrived)
    both_crossed = on_head(both_leaving, ACROSS_X)
    beyond_keep, beyond_arrived = spread_out(
        after(far_end_rows, own_keep, both_leaving),
        waits_for=(beside(own_keep, far_end_rows),),
    )
    beyond_leaving = added_half(here, False, beyond_keep, beyond_arrived)
    beyond_crossed = on_head(beyond_leaving, ACROSS_X)
    own_chip = added_pieces(
        here,
        own_keep,
        after(own_arrived[0], beyond_leaving),
        2,
        waits_for=(beside(own_rows, both_crossed),),
    )
    own_crossed = [
        across_home(after(part, earlier))
        for part, earlier in zip(own_chip, (both_crossed, beyond_crossed))
    ]
    first_sum, second_sum = added_halves(here, both_keep, both_arrived, both_crossed)

    def far(at):
        return 3 - at

    def end(at):
        return at ^ 1

    def beyond(at):
        return (3 - at) ^ 1

    first_home = sent_home(first_sum, home_pairs(far, False), home_pairs(end, True))
    second_home = sent_home(second_sum, home_pairs(far, True), home_pairs(end, False))
    beyond_sum = added_half(
        here, True, beyond_keep, beyond_arrived, beyond_crossed
    )
    beyond_home = [sent_home(beyond_sum, home_pairs(beyond, turned)) for turned in (False, True)]
    own_home = joined(
        here, own_chip, own_crossed, waits_for=(beside(own_keep, own_crossed[0]),)
    )

    is_middle = jnp.logical_or(plane == 1, plane == 2)
    near_side = chip == plane // 2
    straight = jnp.where(is_middle, first_home, jnp.where(near_side, second_home, beyond_home[0]))
    turned = jnp.where(is_middle, second_home, jnp.where(near_side, first_home, beyond_home[1]))
    return jnp.where(
        jnp.logical_and(is_middle, near_side),
        own_home,
        jnp.where(
            chip == 0,
            jnp.concatenate([straight, turned], axis=0),
            jnp.concatenate([turned, straight], axis=0),
        ),
    )


def solution(mesh):
    line, width = mesh.shape["samp"], mesh.shape["head"]
    paired = line == 4 and width == 4 and mesh.shape["groups"] == 2
    on_device = inward_plan if paired else general_plan

    placed = (
        P(("groups", "samp"), None, "head"),
        P("groups"),
        P("groups"),
        P("head", None),
        P(("groups", "samp")),
        P(None, ("groups", "samp"), "head"),
        P(None, ("groups", "samp"), "head"),
        P("head", "samp"),
    )
    return jax.shard_map(
        on_device,
        mesh=mesh,
        in_specs=placed,
        out_specs=P(None, ("groups", "samp"), "head"),
        check_vma=False,
    )
```

```python
import math

import jax
import jax.numpy as jnp
from jax import lax
from jax.experimental import pallas as pl
from jax.experimental.pallas import tpu as pltpu
from jax.sharding import PartitionSpec as P

HD = 128
GQA = 5


masked_score = -1e30


def prompt_partial(queries, page_block, length):
    row_count = queries.shape[0]
    groups = page_block.shape[0] // (2 * HD)
    score_scale = 1.0 / math.sqrt(HD)
    query_heads = queries.reshape(row_count, groups, GQA, HD)
    page_heads = page_block.reshape(groups, 2, HD, page_block.shape[1])
    scores = (
        jnp.einsum(
            "rgjd,gdl->grjl", query_heads, page_heads[:, 0], preferred_element_type=jnp.float32
        )
        * score_scale
    )
    usable = lax.broadcasted_iota(jnp.int32, scores.shape, 3) < length
    peak_score = jnp.max(jnp.where(usable, scores, masked_score), axis=3)
    weights = jnp.where(usable, jnp.exp(scores - peak_score[..., None]), 0.0)
    totals = jnp.sum(weights, axis=3)
    summed = jnp.einsum(
        "grjl,gdl->grjd",
        weights.astype(jnp.bfloat16),
        page_heads[:, 1],
        preferred_element_type=jnp.float32,
    )
    summed = jnp.transpose(summed, (1, 0, 2, 3)).reshape(row_count, groups * GQA * HD)
    peak_score = jnp.transpose(peak_score, (1, 0, 2)).reshape(row_count, groups * GQA)
    totals = jnp.transpose(totals, (1, 0, 2)).reshape(row_count, groups * GQA)
    return (summed, peak_score, totals)


def general_plan(
    prompt_states,
    prompt_lengths,
    prompt_owner,
    kv_weight,
    sampler_prompts,
    step_queries,
    step_kv,
    out_weight,
):
    states = prompt_states[0]
    own_pages = lax.psum_scatter(
        lax.dot_general(
            kv_weight, states, (((0,), (1,)), ((), ())), preferred_element_type=jnp.float32
        ).astype(jnp.bfloat16),
        "head",
        scatter_dimension=0,
        tiled=True,
    )
    step_count = step_queries.shape[0]
    row_total = step_queries.shape[1]
    prompt_count = sampler_prompts.shape[0]
    block_rows = row_total // prompt_count
    head_width = step_queries.shape[2]
    groups = own_pages.shape[0] // (2 * HD)
    owner_slots = jnp.take(prompt_owner, sampler_prompts)
    block_lengths = jnp.take(prompt_lengths, sampler_prompts)
    block_queries = [
        step_queries[:, position * block_rows : (position + 1) * block_rows].reshape(
            step_count * block_rows, head_width
        )
        for position in range(prompt_count)
    ]
    library = lax.all_gather(own_pages[None], "samp", axis=0, tiled=True)
    partials = []
    for position in range(prompt_count):
        page_block = lax.dynamic_index_in_dim(library, owner_slots[position], 0, keepdims=False)
        partials.append(
            prompt_partial(block_queries[position], page_block, block_lengths[position])
        )
    prompt_sum = jnp.concatenate(
        [entry[0].reshape(step_count, block_rows, groups, GQA, HD) for entry in partials], axis=1
    )
    prompt_peak = jnp.concatenate(
        [entry[1].reshape(step_count, block_rows, groups, GQA) for entry in partials], axis=1
    )
    prompt_total = jnp.concatenate(
        [entry[2].reshape(step_count, block_rows, groups, GQA) for entry in partials], axis=1
    )
    score_scale = 1.0 / math.sqrt(HD)
    query_all = step_queries.reshape(step_count, row_total, groups, GQA, HD)
    own_cache = step_kv.reshape(step_count, row_total, groups, 2, HD)
    near_scores = (
        jnp.einsum(
            "trgjd,urgd->trgju",
            query_all,
            own_cache[:, :, :, 0],
            preferred_element_type=jnp.float32,
        )
        * score_scale
    )
    causal = lax.broadcasted_iota(jnp.int32, near_scores.shape, 4) <= lax.broadcasted_iota(
        jnp.int32, near_scores.shape, 0
    )
    near_peak = jnp.max(jnp.where(causal, near_scores, masked_score), axis=4)
    near_weights = jnp.where(causal, jnp.exp(near_scores - near_peak[..., None]), 0.0)
    near_total = jnp.sum(near_weights, axis=4)
    near_sum = jnp.einsum(
        "trgju,urgd->trgjd",
        near_weights.astype(jnp.bfloat16),
        own_cache[:, :, :, 1],
        preferred_element_type=jnp.float32,
    )
    peak_all = jnp.maximum(prompt_peak, near_peak)
    far_factor = jnp.exp(prompt_peak - peak_all)
    near_factor = jnp.exp(near_peak - peak_all)
    numerator = prompt_sum * far_factor[..., None] + near_sum * near_factor[..., None]
    denominator = prompt_total * far_factor + near_total * near_factor
    attention = (numerator / denominator[..., None]).astype(jnp.bfloat16)
    attention = attention.reshape(step_count * row_total, groups * GQA * HD)
    terms = jnp.dot(
        attention,
        lax.all_gather(out_weight, "samp", axis=1, tiled=True),
        preferred_element_type=jnp.float32,
    )
    mixed = lax.psum_scatter(
        terms.astype(jnp.bfloat16), "head", scatter_dimension=1, tiled=True
    ).astype(jnp.float32)
    return mixed.astype(jnp.bfloat16).reshape(step_count, row_total, mixed.shape[1])


VMEM = 24 * 1024 * 1024
LARGE_VMEM = 60 * 1024 * 1024

CORE = [(0, 1), (1, 0), (2, 3), (3, 2)]
ACROSS_X = [(0, 2), (2, 0), (1, 3), (3, 1)]
INWARD = [(0, 1), (3, 2)]
MIDDLE = [(1, 2), (2, 1)]


def compiler_params(limit=VMEM):
    return pltpu.CompilerParams(vmem_limit_bytes=limit)


def small_cost():
    return pl.CostEstimate(flops=64, bytes_accessed=64, transcendentals=0)


def project(here, states, weight, masks, cuts):
    features, width = weight.shape[0], weight.shape[1] // 4
    parts = [(low, high - low) for low, high in zip(cuts[:-1], cuts[1:])]

    def body(here_ref, state_hbm, weight_hbm, *rest):
        outs, (state, blocks, state_sems, block_sems) = rest[: 2 * len(parts)], rest[2 * len(parts) :]
        fetches, blocks_in = [], []
        for side in range(2):
            place = here_ref[2] ^ masks[side]
            columns = pl.ds(pl.multiple_of(place * width, width), width)
            blocks_in.append(
                pltpu.make_async_copy(
                    weight_hbm.at[:, columns], blocks.at[side], block_sems.at[side]
                )
            )
        for at, (low, rows) in enumerate(parts):
            fetches.append(
                pltpu.make_async_copy(
                    state_hbm.at[low : low + rows], state.at[low : low + rows], state_sems.at[at]
                )
            )
        blocks_in[0].start()
        fetches[0].start()
        blocks_in[1].start()
        for fetch in fetches[1:]:
            fetch.start()
        for at, (low, rows) in enumerate(parts):
            fetches[at].wait()
            for side in range(2):
                if at == 0:
                    blocks_in[side].wait()
                outs[side * len(parts) + at][...] = jnp.dot(
                    state[low : low + rows], blocks[side], preferred_element_type=jnp.float32
                ).astype(jnp.bfloat16)

    in_hbm = pl.BlockSpec(memory_space=pltpu.HBM)
    in_vmem = pl.BlockSpec(memory_space=pltpu.VMEM)
    outs = pl.pallas_call(
        body,
        in_specs=[pl.BlockSpec(memory_space=pltpu.SMEM), in_hbm, in_hbm],
        out_specs=[in_vmem] * (2 * len(parts)),
        out_shape=[jax.ShapeDtypeStruct((rows, width), jnp.bfloat16) for _, rows in parts] * 2,
        scratch_shapes=[
            pltpu.VMEM(states.shape, jnp.bfloat16),
            pltpu.VMEM((2, features, width), jnp.bfloat16),
            pltpu.SemaphoreType.DMA((len(parts),)),
            pltpu.SemaphoreType.DMA((2,)),
        ],
        compiler_params=compiler_params(LARGE_VMEM),
        cost_estimate=small_cost(),
        name="project",
    )(here, states, weight)
    return outs[: len(parts)], outs[len(parts) :]


def attend(chosen, here, prompts, owners, lengths, queries, news, pages):
    news, new_start = news
    steps, rows, _ = queries.shape
    blocks = prompts.shape[0]
    block_rows = rows // blocks
    new_width = pages[0][0].shape[1]
    groups = new_width // (2 * HD)
    width = groups * GQA * HD
    tokens = sum(part.shape[0] for part in pages[0])
    count = chosen[1] - chosen[0]
    page_parts = [part for page in pages for part in page]
    tiles = 4
    chunk = tokens // tiles
    flat = steps * block_rows
    factor = math.log2(math.e) / math.sqrt(HD)

    def body(here_ref, prompts_ref, owners_ref, lengths_ref, query_hbm, new_hbm, *rest):
        page_refs, rest = rest[: len(page_parts)], rest[len(page_parts) :]
        out_ref, held, query_ref, new_ref, sems = rest
        plane = here_ref[1]

        def run(at, written, used, length):
            query = query_ref[at].reshape(flat, width)
            new = new_ref[at].reshape(flat, new_width)
            shape = (GQA * flat, flat)
            asker = lax.broadcasted_iota(jnp.int32, shape, 0) % flat
            holder = lax.broadcasted_iota(jnp.int32, shape, 1)
            near_ok = jnp.logical_and(asker % block_rows == holder % block_rows, holder <= asker)
            last = (GQA * flat, chunk)
            last_ok = lax.broadcasted_iota(jnp.int32, last, 1) < length - (used - chunk)
            for group in range(groups):
                key = slice(2 * group * HD, (2 * group + 1) * HD)
                value = slice((2 * group + 1) * HD, (2 * group + 2) * HD)
                asked = jnp.concatenate(
                    [
                        query[:, (group * GQA + head) * HD : (group * GQA + head + 1) * HD]
                        for head in range(GQA)
                    ],
                    axis=0,
                )

                def scores(keys):
                    return lax.dot_general(
                        asked, keys, (((1,), (1,)), ((), ())), preferred_element_type=jnp.float32
                    )

                parts = [
                    scores(held[at, tile * chunk : (tile + 1) * chunk, key])
                    for tile in range(used // chunk)
                ]
                parts[-1] = jnp.where(last_ok, parts[-1], masked_score)
                parts.append(jnp.where(near_ok, scores(new[:, key]), masked_score))
                peak = jnp.max(parts[0], axis=1, keepdims=True)
                for part in parts[1:]:
                    peak = jnp.maximum(peak, jnp.max(part, axis=1, keepdims=True))
                total, summed = 0.0, 0.0
                for tile, part in enumerate(parts):
                    weights = jnp.exp2((part - peak) * factor)
                    total = total + jnp.sum(weights, axis=1, keepdims=True)
                    values = (
                        held[at, tile * chunk : (tile + 1) * chunk, value]
                        if tile < len(parts) - 1
                        else new[:, value]
                    )
                    summed = summed + jnp.dot(
                        weights.astype(jnp.bfloat16), values, preferred_element_type=jnp.float32
                    )
                result = (summed / total).astype(jnp.bfloat16)
                for head in range(GQA):
                    column = (group * GQA + head) * HD
                    out_ref[:, written, column : column + HD] = result[
                        head * flat : (head + 1) * flat
                    ].reshape(steps, block_rows, HD)

        for block in range(*chosen):
            at = block - chosen[0]
            mine = slice(block * block_rows, (block + 1) * block_rows)
            pltpu.make_async_copy(
                query_hbm.at[:, mine, :width], query_ref.at[at], sems.at[0, at]
            ).start()
            pltpu.make_async_copy(
                new_hbm.at[:, mine, new_start : new_start + new_width], new_ref.at[at], sems.at[1, at]
            ).start()
            slot, passed = owners_ref[prompts_ref[block]], 0
            for page, place in zip(pages, (plane, plane ^ 1, 3 - plane, (3 - plane) ^ 1)):
                refs = page_refs[passed : passed + len(page)]
                passed += len(page)

                @pl.when(slot == place)
                def _():
                    low = 0
                    for ref in refs:
                        target = held.at[at, low : low + ref.shape[0]]
                        pltpu.make_async_copy(ref, target, sems.at[2, at]).start()
                        low += ref.shape[0]

        @pl.loop(0, count)
        def _(at):
            written = pl.ds(pl.multiple_of(at * block_rows, block_rows), block_rows)
            for kind, buffer in enumerate((query_ref, new_ref, held)):
                whole = buffer.at[at]
                pltpu.make_async_copy(whole, whole, sems.at[kind, at]).wait()
            length = lengths_ref[prompts_ref[chosen[0] + at]]
            for used in range(1, tiles + 1):
                enough = length > (used - 1) * chunk
                if used < tiles:
                    enough = jnp.logical_and(enough, length <= used * chunk)

                @pl.when(enough)
                def _():
                    run(at, written, used * chunk, length)

    in_vmem, in_smem, in_hbm = (
        pl.BlockSpec(memory_space=space) for space in (pltpu.VMEM, pltpu.SMEM, pltpu.HBM)
    )
    return pl.pallas_call(
        body,
        in_specs=[in_smem] * 4 + [in_hbm] * (2 + len(page_parts)),
        out_specs=in_vmem,
        out_shape=jax.ShapeDtypeStruct(
            (steps, count * block_rows, width), jnp.bfloat16
        ),
        scratch_shapes=[
            pltpu.VMEM((count, tokens, new_width), jnp.bfloat16),
            pltpu.VMEM((count, steps, block_rows, width), jnp.bfloat16),
            pltpu.VMEM((count, steps, block_rows, new_width), jnp.bfloat16),
            pltpu.SemaphoreType.DMA((3, count)),
        ],
        compiler_params=compiler_params(40 * 1024 * 1024),
        cost_estimate=small_cost(),
        name="attend",
    )(here, prompts, owners, lengths, queries, news, *page_parts)


def spread(here, blocks, own_weight, moved_weights, waits_for):
    count, moved_count = len(blocks), len(moved_weights)
    steps, _, features = blocks[0].shape
    columns = own_weight.shape[1]
    tile = 256 if columns % 256 == 0 else columns
    ends = [0]
    for block in blocks:
        ends.append(ends[-1] + block.shape[1])
    places = [slice(low, high) for low, high in zip(ends[:-1], ends[1:])]

    def body(here_ref, *refs):
        row_refs, own_ref, refs = refs[:count], refs[count], refs[count + 1 :]
        moved_refs, refs = refs[:moved_count], refs[moved_count + len(waits_for) :]
        keep_ref, send_refs, taken_ref = refs[0], refs[1:-1], refs[-1]
        for ref, place in zip(row_refs, places):
            flat = slice(steps * place.start, steps * place.stop)
            taken_ref[flat] = ref[...].reshape(flat.stop - flat.start, features)
        taken = taken_ref[...]
        pieces = []
        for low, other, part in moved_weights:
            start = (here_ref[0] ^ other) * (features // 2) + low
            pieces.append(taken_ref[:, pl.ds(pl.multiple_of(start, 128), part.shape[0])])
        keeps_own = (here_ref[1] ^ here_ref[2]) % 2 == 0
        for column in range(0, columns, tile):
            part = slice(column, column + tile)
            own = jnp.dot(taken, own_ref[:, part], preferred_element_type=jnp.float32)
            moved = 0.0
            for piece, moved_ref in zip(pieces, moved_refs):
                moved = moved + jnp.dot(
                    piece, moved_ref[:, part], preferred_element_type=jnp.float32
                )
            keep = jnp.where(keeps_own, own, moved).astype(jnp.bfloat16)
            send = jnp.where(keeps_own, moved, own).astype(jnp.bfloat16)
            for place, send_ref in zip(places, send_refs):
                flat = slice(steps * place.start, steps * place.stop)
                shape = (steps, place.stop - place.start, tile)
                keep_ref[:, place, part] = keep[flat].reshape(shape)
                send_ref[:, :, part] = send[flat].reshape(shape)

    in_vmem = pl.BlockSpec(memory_space=pltpu.VMEM)
    out_rows = [ends[-1], *[block.shape[1] for block in blocks]]
    keep, *sends = pl.pallas_call(
        body,
        in_specs=[pl.BlockSpec(memory_space=pltpu.SMEM)] + [in_vmem] * (count + 1 + moved_count)
        + [pl.BlockSpec(memory_space=pltpu.HBM)] * len(waits_for),
        out_specs=[in_vmem] * (1 + count),
        out_shape=[jax.ShapeDtypeStruct((steps, rows, columns), jnp.bfloat16) for rows in out_rows],
        scratch_shapes=[pltpu.VMEM((steps * ends[-1], features), jnp.bfloat16)],
        compiler_params=compiler_params(),
        cost_estimate=small_cost(),
        name="spread",
    )(here, *blocks, own_weight, *[part for _, _, part in moved_weights], *waits_for)
    return keep, sends


def run_small(body, name, here, operands, out_shape, outs=1, limit=VMEM, waits_for=()):
    in_vmem = pl.BlockSpec(memory_space=pltpu.VMEM)

    def whole(*refs):
        body(*refs[: 1 + len(operands)], *refs[1 + len(operands) + len(waits_for) :])

    return pl.pallas_call(
        whole,
        in_specs=[pl.BlockSpec(memory_space=pltpu.SMEM)]
        + [in_vmem] * len(operands)
        + [pl.BlockSpec(memory_space=pltpu.HBM)] * len(waits_for),
        out_specs=[in_vmem] * outs,
        out_shape=[jax.ShapeDtypeStruct(out_shape, jnp.bfloat16)] * outs,
        compiler_params=compiler_params(limit),
        cost_estimate=small_cost(),
        name=name,
    )(here, *operands, *waits_for)


def added(here, *parts, limit=VMEM):
    def body(_, *refs):
        total = refs[0][...].astype(jnp.float32)
        for ref in refs[1:-1]:
            total = total + ref[...].astype(jnp.float32)
        refs[-1][...] = total.astype(jnp.bfloat16)

    return run_small(body, "added", here, parts, parts[0].shape, limit=limit)[0]


def added_pieces(here, one, two, pieces, waits_for):
    steps, rows, columns = one.shape
    piece = rows // pieces

    def body(_, one_ref, two_ref, *outs):
        total = one_ref[...].astype(jnp.float32) + two_ref[...].astype(jnp.float32)
        total = total.astype(jnp.bfloat16)
        for at, out in enumerate(outs):
            out[...] = total[:, at * piece : (at + 1) * piece]

    shape = (steps, piece, columns)
    return run_small(body, "added_pieces", here, (one, two), shape, pieces, waits_for=waits_for)


def joined(here, ones, twos, waits_for):
    steps, piece, columns = ones[0].shape
    count = len(ones)

    def body(_, *refs):
        for at in range(count):
            total = refs[at][...].astype(jnp.float32) + refs[count + at][...].astype(jnp.float32)
            refs[-1][:, at * piece : (at + 1) * piece] = total.astype(jnp.bfloat16)

    shape = (steps, count * piece, columns)
    return run_small(body, "joined", here, (*ones, *twos), shape, waits_for=waits_for)[0]


def stacked(here, *parts, waits_for):
    rows = [part.shape[0] for part in parts]

    def body(_, *refs):
        for at, ref in enumerate(refs[:-1]):
            refs[-1][sum(rows[:at]) : sum(rows[: at + 1])] = ref[...]

    shape = (sum(rows), *parts[0].shape[1:])
    return run_small(body, "stacked", here, parts, shape, waits_for=waits_for)[0]


def added_half(here, mine, keep, sends, crossed=None):
    steps, rows, columns = keep.shape
    half, count = steps // 2, len(sends)
    ends = [sum(send.shape[1] for send in sends[:at]) for at in range(count + 1)]

    def body(here_ref, keep_ref, *refs):
        chip = here_ref[2] // 2
        taken = pl.ds((chip if mine else 1 - chip) * half, half)
        for at in range(count):
            place = slice(ends[at], ends[at + 1])
            total = keep_ref[taken, place].astype(jnp.float32) + refs[at][taken].astype(jnp.float32)
            if crossed is not None:
                total = total + refs[count][:, place].astype(jnp.float32)
            refs[-1][:, place] = total.astype(jnp.bfloat16)

    operands = (keep, *sends) if crossed is None else (keep, *sends, crossed)
    return run_small(body, "added_half", here, operands, (half, rows, columns))[0]


def added_halves(here, keep, sends, crossed):
    steps, rows, columns = keep.shape
    half, piece = steps // 2, rows // 2

    def body(here_ref, keep_ref, far_ref, end_ref, crossed_ref, first_ref, second_ref):
        chip = here_ref[2] // 2
        taken = pl.ds(chip * half, half)
        total = keep_ref[taken].astype(jnp.float32) + crossed_ref[...].astype(jnp.float32)
        far = (total[:, :piece] + far_ref[taken].astype(jnp.float32)).astype(jnp.bfloat16)
        end = (total[:, piece:] + end_ref[taken].astype(jnp.float32)).astype(jnp.bfloat16)
        at_home = here_ref[1] // 2 == chip

        @pl.when(at_home)
        def _():
            first_ref[...] = far
            second_ref[...] = end

        @pl.when(jnp.logical_not(at_home))
        def _():
            first_ref[...] = end
            second_ref[...] = far

    shape = (half, piece, columns)
    return run_small(body, "added_halves", here, (keep, *sends, crossed), shape, 2)


def after(value, *others):
    return lax.optimization_barrier((value, *others))[0]


def home_pairs(target, turned):
    pairs = []
    for source in (1, 2):
        side = source // 2
        chip = 1 - side if turned else side
        for at in range(2):
            pairs.append((source * 4 + 2 * chip + at, target(source) * 4 + 2 * side + at))
    return pairs


def sent_home(value, *pairs):
    return lax.ppermute(value, ("samp", "head"), [pair for part in pairs for pair in part])


def across_home(value):
    pairs = [
        (source * 4 + 2 * (1 - source // 2) + at, source * 4 + 2 * (source // 2) + at)
        for source in (1, 2)
        for at in range(2)
    ]
    return lax.ppermute(value, ("samp", "head"), pairs)


def inward_plan(
    prompt_states,
    prompt_lengths,
    prompt_owner,
    kv_weight,
    sampler_prompts,
    step_queries,
    step_kv,
    out_weight,
):
    group, plane, head = (lax.axis_index(name) for name in ("groups", "samp", "head"))
    chip = head // 2
    here = jnp.stack([group, plane, head]).astype(jnp.int32)

    def on_samp(value, pairs):
        return lax.ppermute(value, "samp", pairs)

    def on_head(value, pairs):
        return lax.ppermute(value, "head", pairs)

    def hopped(*values):
        token = here
        for value in values:
            token = on_head(after(token, *value), CORE)
        return token

    def beside(value, *others):
        return on_head(after(value, *others), CORE)

    states = prompt_states[0]
    tokens = states.shape[0]
    cuts = [0, tokens * 7 // 16, tokens]
    sent, kept = project(here, states, kv_weight, (3, 2), cuts)

    half = out_weight.shape[0] // 2
    weight_cuts = [0, half * 2 // 5, half]

    def weight_part(at, *others):
        low, size = weight_cuts[at], weight_cuts[at + 1] - weight_cuts[at]
        return lax.dynamic_slice_in_dim(after(out_weight, *others), group * half + low, size, 0)

    def swapped(part):
        return lax.ppermute(part, "groups", [(0, 1), (1, 0)])

    weight_0 = on_samp(weight_part(0, sent[0]), INWARD)
    leaving_first = added(here, kept[0], on_head(sent[0], CORE), limit=32 * 1024 * 1024)
    leaving_second = added(here, kept[1], after(on_head(sent[1], CORE), leaving_first), limit=32 * 1024 * 1024)
    crossed_first = on_head(leaving_first, ACROSS_X)
    crossed_second = on_head(leaving_second, ACROSS_X)
    sent, kept = project(
        here, after(states, leaving_first, leaving_second), kv_weight, (1, 0), cuts
    )
    sent = [on_head(value, CORE) for value in sent]
    first = added(hopped((crossed_first,)), kept[0], sent[0], crossed_first, limit=32 * 1024 * 1024)
    end_first = on_samp(after(first, weight_0), INWARD)
    far_first = on_samp(first, MIDDLE)
    second = added(here, kept[1], sent[1], crossed_second, limit=32 * 1024 * 1024)
    end_second = on_samp(second, INWARD)
    far_second = on_samp(second, MIDDLE)
    end_page = stacked(
        here, end_first, end_second, waits_for=(beside(leaving_first, far_first, end_first),)
    )
    moved_0 = swapped(weight_0)
    far_end_page = on_samp(after(end_page, far_second), MIDDLE)
    pages = ((first, second), (end_page,), (far_first, far_second), (far_end_page,))
    end_prompts = on_samp(after(sampler_prompts, second), INWARD)
    weight_1 = on_samp(after(weight_part(1, first), end_second, end_prompts), INWARD)
    asked = jnp.concatenate([after(step_queries, first), step_kv], axis=2)
    end_asked = on_samp(after(asked, weight_1), INWARD)
    parts = ((weight_0, moved_0), (weight_1, swapped(weight_1)))
    moved_weights = [
        (low, side, part[side]) for side in range(2) for low, part in zip(weight_cuts, parts)
    ]

    def attended(place, chosen, prompts, queries, news):
        rows = attend(
            chosen, place, prompts, prompt_owner, prompt_lengths, queries, news, pages
        )
        return rows, on_samp(rows, MIDDLE)

    def spread_out(*blocks, waits_for=()):
        keep, sends = spread(here, blocks, out_weight, moved_weights, waits_for)
        return keep, [on_head(send, CORE) for send in sends]

    blocks = sampler_prompts.shape[0]
    own_rows, far_own_rows = attended(
        here, (0, blocks), sampler_prompts, after(step_queries, moved_0), (step_kv, 0)
    )
    end_rows, far_end_rows = attended(
        here,
        (0, blocks),
        end_prompts,
        after(end_asked, own_rows),
        (end_asked, step_queries.shape[2]),
    )
    both_keep, both_arrived = spread_out(far_own_rows, end_rows)
    own_keep, own_arrived = spread_out(after(own_rows, both_keep))
    both_leaving = added_half(here, False, both_keep, both_arrived)
    both_crossed = on_head(both_leaving, ACROSS_X)
    beyond_keep, beyond_arrived = spread_out(
        after(far_end_rows, own_keep, both_leaving),
        waits_for=(beside(own_keep, far_end_rows),),
    )
    beyond_leaving = added_half(here, False, beyond_keep, beyond_arrived)
    beyond_crossed = on_head(beyond_leaving, ACROSS_X)
    own_chip = added_pieces(
        here,
        own_keep,
        after(own_arrived[0], beyond_leaving),
        2,
        waits_for=(beside(own_rows, both_crossed),),
    )
    own_crossed = [
        across_home(after(part, earlier))
        for part, earlier in zip(own_chip, (both_crossed, beyond_crossed))
    ]
    first_sum, second_sum = added_halves(here, both_keep, both_arrived, both_crossed)

    def far(at):
        return 3 - at

    def end(at):
        return at ^ 1

    def beyond(at):
        return (3 - at) ^ 1

    first_home = sent_home(first_sum, home_pairs(far, False), home_pairs(end, True))
    second_home = sent_home(second_sum, home_pairs(far, True), home_pairs(end, False))
    beyond_sum = added_half(
        here, True, beyond_keep, beyond_arrived, beyond_crossed
    )
    beyond_home = [sent_home(beyond_sum, home_pairs(beyond, turned)) for turned in (False, True)]
    own_home = joined(
        here, own_chip, own_crossed, waits_for=(beside(own_keep, own_crossed[0]),)
    )

    is_middle = jnp.logical_or(plane == 1, plane == 2)
    near_side = chip == plane // 2
    straight = jnp.where(is_middle, first_home, jnp.where(near_side, second_home, beyond_home[0]))
    turned = jnp.where(is_middle, second_home, jnp.where(near_side, first_home, beyond_home[1]))
    return jnp.where(
        jnp.logical_and(is_middle, near_side),
        own_home,
        jnp.where(
            chip == 0,
            jnp.concatenate([straight, turned], axis=0),
            jnp.concatenate([turned, straight], axis=0),
        ),
    )


def solution(mesh):
    line, width = mesh.shape["samp"], mesh.shape["head"]
    paired = line == 4 and width == 4 and mesh.shape["groups"] == 2
    on_device = inward_plan if paired else general_plan

    placed = (
        P(("groups", "samp"), None, "head"),
        P("groups"),
        P("groups"),
        P("head", None),
        P(("groups", "samp")),
        P(None, ("groups", "samp"), "head"),
        P(None, ("groups", "samp"), "head"),
        P("head", "samp"),
    )
    return jax.shard_map(
        on_device,
        mesh=mesh,
        in_specs=placed,
        out_specs=P(None, ("groups", "samp"), "head"),
        check_vma=False,
    )
```

```python
import math

import jax
import jax.numpy as jnp
from jax import lax
from jax.experimental import pallas as pl
from jax.experimental.pallas import tpu as pltpu
from jax.sharding import PartitionSpec as P

HD = 128
GQA = 5


masked_score = -1e30


def prompt_partial(queries, page_block, length):
    row_count = queries.shape[0]
    groups = page_block.shape[0] // (2 * HD)
    score_scale = 1.0 / math.sqrt(HD)
    query_heads = queries.reshape(row_count, groups, GQA, HD)
    page_heads = page_block.reshape(groups, 2, HD, page_block.shape[1])
    scores = (
        jnp.einsum(
            "rgjd,gdl->grjl", query_heads, page_heads[:, 0], preferred_element_type=jnp.float32
        )
        * score_scale
    )
    usable = lax.broadcasted_iota(jnp.int32, scores.shape, 3) < length
    peak_score = jnp.max(jnp.where(usable, scores, masked_score), axis=3)
    weights = jnp.where(usable, jnp.exp(scores - peak_score[..., None]), 0.0)
    totals = jnp.sum(weights, axis=3)
    summed = jnp.einsum(
        "grjl,gdl->grjd",
        weights.astype(jnp.bfloat16),
        page_heads[:, 1],
        preferred_element_type=jnp.float32,
    )
    summed = jnp.transpose(summed, (1, 0, 2, 3)).reshape(row_count, groups * GQA * HD)
    peak_score = jnp.transpose(peak_score, (1, 0, 2)).reshape(row_count, groups * GQA)
    totals = jnp.transpose(totals, (1, 0, 2)).reshape(row_count, groups * GQA)
    return (summed, peak_score, totals)


def general_plan(
    prompt_states,
    prompt_lengths,
    prompt_owner,
    kv_weight,
    sampler_prompts,
    step_queries,
    step_kv,
    out_weight,
):
    states = prompt_states[0]
    own_pages = lax.psum_scatter(
        lax.dot_general(
            kv_weight, states, (((0,), (1,)), ((), ())), preferred_element_type=jnp.float32
        ).astype(jnp.bfloat16),
        "head",
        scatter_dimension=0,
        tiled=True,
    )
    step_count = step_queries.shape[0]
    row_total = step_queries.shape[1]
    prompt_count = sampler_prompts.shape[0]
    block_rows = row_total // prompt_count
    head_width = step_queries.shape[2]
    groups = own_pages.shape[0] // (2 * HD)
    owner_slots = jnp.take(prompt_owner, sampler_prompts)
    block_lengths = jnp.take(prompt_lengths, sampler_prompts)
    block_queries = [
        step_queries[:, position * block_rows : (position + 1) * block_rows].reshape(
            step_count * block_rows, head_width
        )
        for position in range(prompt_count)
    ]
    library = lax.all_gather(own_pages[None], "samp", axis=0, tiled=True)
    partials = []
    for position in range(prompt_count):
        page_block = lax.dynamic_index_in_dim(library, owner_slots[position], 0, keepdims=False)
        partials.append(
            prompt_partial(block_queries[position], page_block, block_lengths[position])
        )
    prompt_sum = jnp.concatenate(
        [entry[0].reshape(step_count, block_rows, groups, GQA, HD) for entry in partials], axis=1
    )
    prompt_peak = jnp.concatenate(
        [entry[1].reshape(step_count, block_rows, groups, GQA) for entry in partials], axis=1
    )
    prompt_total = jnp.concatenate(
        [entry[2].reshape(step_count, block_rows, groups, GQA) for entry in partials], axis=1
    )
    score_scale = 1.0 / math.sqrt(HD)
    query_all = step_queries.reshape(step_count, row_total, groups, GQA, HD)
    own_cache = step_kv.reshape(step_count, row_total, groups, 2, HD)
    near_scores = (
        jnp.einsum(
            "trgjd,urgd->trgju",
            query_all,
            own_cache[:, :, :, 0],
            preferred_element_type=jnp.float32,
        )
        * score_scale
    )
    causal = lax.broadcasted_iota(jnp.int32, near_scores.shape, 4) <= lax.broadcasted_iota(
        jnp.int32, near_scores.shape, 0
    )
    near_peak = jnp.max(jnp.where(causal, near_scores, masked_score), axis=4)
    near_weights = jnp.where(causal, jnp.exp(near_scores - near_peak[..., None]), 0.0)
    near_total = jnp.sum(near_weights, axis=4)
    near_sum = jnp.einsum(
        "trgju,urgd->trgjd",
        near_weights.astype(jnp.bfloat16),
        own_cache[:, :, :, 1],
        preferred_element_type=jnp.float32,
    )
    peak_all = jnp.maximum(prompt_peak, near_peak)
    far_factor = jnp.exp(prompt_peak - peak_all)
    near_factor = jnp.exp(near_peak - peak_all)
    numerator = prompt_sum * far_factor[..., None] + near_sum * near_factor[..., None]
    denominator = prompt_total * far_factor + near_total * near_factor
    attention = (numerator / denominator[..., None]).astype(jnp.bfloat16)
    attention = attention.reshape(step_count * row_total, groups * GQA * HD)
    terms = jnp.dot(
        attention,
        lax.all_gather(out_weight, "samp", axis=1, tiled=True),
        preferred_element_type=jnp.float32,
    )
    mixed = lax.psum_scatter(
        terms.astype(jnp.bfloat16), "head", scatter_dimension=1, tiled=True
    ).astype(jnp.float32)
    return mixed.astype(jnp.bfloat16).reshape(step_count, row_total, mixed.shape[1])


VMEM = 24 * 1024 * 1024
LARGE_VMEM = 60 * 1024 * 1024

CORE = [(0, 1), (1, 0), (2, 3), (3, 2)]
ACROSS_X = [(0, 2), (2, 0), (1, 3), (3, 1)]
INWARD = [(0, 1), (3, 2)]
MIDDLE = [(1, 2), (2, 1)]


def compiler_params(limit=VMEM):
    return pltpu.CompilerParams(vmem_limit_bytes=limit)


def small_cost():
    return pl.CostEstimate(flops=64, bytes_accessed=64, transcendentals=0)


def project(here, states, weight, masks, cuts):
    features, width = weight.shape[0], weight.shape[1] // 4
    parts = [(low, high - low) for low, high in zip(cuts[:-1], cuts[1:])]

    def body(here_ref, state_hbm, weight_hbm, *rest):
        outs, (state, blocks, state_sems, block_sems) = rest[: 2 * len(parts)], rest[2 * len(parts) :]
        fetches, blocks_in = [], []
        for side in range(2):
            place = here_ref[2] ^ masks[side]
            columns = pl.ds(pl.multiple_of(place * width, width), width)
            blocks_in.append(
                pltpu.make_async_copy(
                    weight_hbm.at[:, columns], blocks.at[side], block_sems.at[side]
                )
            )
        for at, (low, rows) in enumerate(parts):
            fetches.append(
                pltpu.make_async_copy(
                    state_hbm.at[low : low + rows], state.at[low : low + rows], state_sems.at[at]
                )
            )
        blocks_in[0].start()
        fetches[0].start()
        blocks_in[1].start()
        for fetch in fetches[1:]:
            fetch.start()
        for at, (low, rows) in enumerate(parts):
            fetches[at].wait()
            for side in range(2):
                if at == 0:
                    blocks_in[side].wait()
                outs[side * len(parts) + at][...] = jnp.dot(
                    state[low : low + rows], blocks[side], preferred_element_type=jnp.float32
                ).astype(jnp.bfloat16)

    in_hbm = pl.BlockSpec(memory_space=pltpu.HBM)
    in_vmem = pl.BlockSpec(memory_space=pltpu.VMEM)
    outs = pl.pallas_call(
        body,
        in_specs=[pl.BlockSpec(memory_space=pltpu.SMEM), in_hbm, in_hbm],
        out_specs=[in_vmem] * (2 * len(parts)),
        out_shape=[jax.ShapeDtypeStruct((rows, width), jnp.bfloat16) for _, rows in parts] * 2,
        scratch_shapes=[
            pltpu.VMEM(states.shape, jnp.bfloat16),
            pltpu.VMEM((2, features, width), jnp.bfloat16),
            pltpu.SemaphoreType.DMA((len(parts),)),
            pltpu.SemaphoreType.DMA((2,)),
        ],
        compiler_params=compiler_params(LARGE_VMEM),
        cost_estimate=small_cost(),
        name="project",
    )(here, states, weight)
    return outs[: len(parts)], outs[len(parts) :]


def attend(chosen, here, prompts, owners, lengths, queries, news, pages):
    news, new_start = news
    steps, rows, _ = queries.shape
    blocks = prompts.shape[0]
    block_rows = rows // blocks
    new_width = pages[0][0].shape[1]
    groups = new_width // (2 * HD)
    width = groups * GQA * HD
    tokens = sum(part.shape[0] for part in pages[0])
    count = chosen[1] - chosen[0]
    page_parts = [part for page in pages for part in page]
    tiles = 4
    chunk = tokens // tiles
    flat = steps * block_rows
    factor = math.log2(math.e) / math.sqrt(HD)

    def body(here_ref, prompts_ref, owners_ref, lengths_ref, query_hbm, new_hbm, *rest):
        page_refs, rest = rest[: len(page_parts)], rest[len(page_parts) :]
        out_ref, held, query_ref, new_ref, sems = rest
        plane = here_ref[1]

        def run(at, written, used, length):
            query = query_ref[at].reshape(flat, width)
            new = new_ref[at].reshape(flat, new_width)
            shape = (GQA * flat, flat)
            asker = lax.broadcasted_iota(jnp.int32, shape, 0) % flat
            holder = lax.broadcasted_iota(jnp.int32, shape, 1)
            near_ok = jnp.logical_and(asker % block_rows == holder % block_rows, holder <= asker)
            last = (GQA * flat, chunk)
            last_ok = lax.broadcasted_iota(jnp.int32, last, 1) < length - (used - chunk)
            for group in range(groups):
                key = slice(2 * group * HD, (2 * group + 1) * HD)
                value = slice((2 * group + 1) * HD, (2 * group + 2) * HD)
                asked = jnp.concatenate(
                    [
                        query[:, (group * GQA + head) * HD : (group * GQA + head + 1) * HD]
                        for head in range(GQA)
                    ],
                    axis=0,
                )

                def scores(keys):
                    return lax.dot_general(
                        asked, keys, (((1,), (1,)), ((), ())), preferred_element_type=jnp.float32
                    )

                parts = [
                    scores(held[at, tile * chunk : (tile + 1) * chunk, key])
                    for tile in range(used // chunk)
                ]
                parts[-1] = jnp.where(last_ok, parts[-1], masked_score)
                parts.append(jnp.where(near_ok, scores(new[:, key]), masked_score))
                peak = jnp.max(parts[0], axis=1, keepdims=True)
                for part in parts[1:]:
                    peak = jnp.maximum(peak, jnp.max(part, axis=1, keepdims=True))
                total, summed = 0.0, 0.0
                for tile, part in enumerate(parts):
                    weights = jnp.exp2((part - peak) * factor)
                    total = total + jnp.sum(weights, axis=1, keepdims=True)
                    values = (
                        held[at, tile * chunk : (tile + 1) * chunk, value]
                        if tile < len(parts) - 1
                        else new[:, value]
                    )
                    summed = summed + jnp.dot(
                        weights.astype(jnp.bfloat16), values, preferred_element_type=jnp.float32
                    )
                result = (summed / total).astype(jnp.bfloat16)
                for head in range(GQA):
                    column = (group * GQA + head) * HD
                    out_ref[:, written, column : column + HD] = result[
                        head * flat : (head + 1) * flat
                    ].reshape(steps, block_rows, HD)

        for block in range(*chosen):
            at = block - chosen[0]
            mine = slice(block * block_rows, (block + 1) * block_rows)
            pltpu.make_async_copy(
                query_hbm.at[:, mine, :width], query_ref.at[at], sems.at[0, at]
            ).start()
            pltpu.make_async_copy(
                new_hbm.at[:, mine, new_start : new_start + new_width], new_ref.at[at], sems.at[1, at]
            ).start()
            slot, passed = owners_ref[prompts_ref[block]], 0
            for page, place in zip(pages, (plane, plane ^ 1, 3 - plane, (3 - plane) ^ 1)):
                refs = page_refs[passed : passed + len(page)]
                passed += len(page)

                @pl.when(slot == place)
                def _():
                    low = 0
                    for ref in refs:
                        target = held.at[at, low : low + ref.shape[0]]
                        pltpu.make_async_copy(ref, target, sems.at[2, at]).start()
                        low += ref.shape[0]

        @pl.loop(0, count)
        def _(at):
            written = pl.ds(pl.multiple_of(at * block_rows, block_rows), block_rows)
            for kind, buffer in enumerate((query_ref, new_ref, held)):
                whole = buffer.at[at]
                pltpu.make_async_copy(whole, whole, sems.at[kind, at]).wait()
            length = lengths_ref[prompts_ref[chosen[0] + at]]
            for used in range(1, tiles + 1):
                enough = length > (used - 1) * chunk
                if used < tiles:
                    enough = jnp.logical_and(enough, length <= used * chunk)

                @pl.when(enough)
                def _():
                    run(at, written, used * chunk, length)

    in_vmem, in_smem, in_hbm = (
        pl.BlockSpec(memory_space=space) for space in (pltpu.VMEM, pltpu.SMEM, pltpu.HBM)
    )
    return pl.pallas_call(
        body,
        in_specs=[in_smem] * 4 + [in_hbm] * (2 + len(page_parts)),
        out_specs=in_vmem,
        out_shape=jax.ShapeDtypeStruct(
            (steps, count * block_rows, width), jnp.bfloat16
        ),
        scratch_shapes=[
            pltpu.VMEM((count, tokens, new_width), jnp.bfloat16),
            pltpu.VMEM((count, steps, block_rows, width), jnp.bfloat16),
            pltpu.VMEM((count, steps, block_rows, new_width), jnp.bfloat16),
            pltpu.SemaphoreType.DMA((3, count)),
        ],
        compiler_params=compiler_params(40 * 1024 * 1024),
        cost_estimate=small_cost(),
        name="attend",
    )(here, prompts, owners, lengths, queries, news, *page_parts)


def spread(here, blocks, own_weight, moved_weights, waits_for):
    count, moved_count = len(blocks), len(moved_weights)
    steps, _, features = blocks[0].shape
    columns = own_weight.shape[1]
    tile = 256 if columns % 256 == 0 else columns
    ends = [0]
    for block in blocks:
        ends.append(ends[-1] + block.shape[1])
    places = [slice(low, high) for low, high in zip(ends[:-1], ends[1:])]

    def body(here_ref, *refs):
        row_refs, own_ref, refs = refs[:count], refs[count], refs[count + 1 :]
        moved_refs, refs = refs[:moved_count], refs[moved_count + len(waits_for) :]
        keep_ref, send_refs, taken_ref = refs[0], refs[1:-1], refs[-1]
        for ref, place in zip(row_refs, places):
            flat = slice(steps * place.start, steps * place.stop)
            taken_ref[flat] = ref[...].reshape(flat.stop - flat.start, features)
        taken = taken_ref[...]
        pieces = []
        for low, other, part in moved_weights:
            start = (here_ref[0] ^ other) * (features // 2) + low
            pieces.append(taken_ref[:, pl.ds(pl.multiple_of(start, 128), part.shape[0])])
        keeps_own = (here_ref[1] ^ here_ref[2]) % 2 == 0
        for column in range(0, columns, tile):
            part = slice(column, column + tile)
            own = jnp.dot(taken, own_ref[:, part], preferred_element_type=jnp.float32)
            moved = 0.0
            for piece, moved_ref in zip(pieces, moved_refs):
                moved = moved + jnp.dot(
                    piece, moved_ref[:, part], preferred_element_type=jnp.float32
                )
            keep = jnp.where(keeps_own, own, moved).astype(jnp.bfloat16)
            send = jnp.where(keeps_own, moved, own).astype(jnp.bfloat16)
            for place, send_ref in zip(places, send_refs):
                flat = slice(steps * place.start, steps * place.stop)
                shape = (steps, place.stop - place.start, tile)
                keep_ref[:, place, part] = keep[flat].reshape(shape)
                send_ref[:, :, part] = send[flat].reshape(shape)

    in_vmem = pl.BlockSpec(memory_space=pltpu.VMEM)
    out_rows = [ends[-1], *[block.shape[1] for block in blocks]]
    keep, *sends = pl.pallas_call(
        body,
        in_specs=[pl.BlockSpec(memory_space=pltpu.SMEM)] + [in_vmem] * (count + 1 + moved_count)
        + [pl.BlockSpec(memory_space=pltpu.HBM)] * len(waits_for),
        out_specs=[in_vmem] * (1 + count),
        out_shape=[jax.ShapeDtypeStruct((steps, rows, columns), jnp.bfloat16) for rows in out_rows],
        scratch_shapes=[pltpu.VMEM((steps * ends[-1], features), jnp.bfloat16)],
        compiler_params=compiler_params(),
        cost_estimate=small_cost(),
        name="spread",
    )(here, *blocks, own_weight, *[part for _, _, part in moved_weights], *waits_for)
    return keep, sends


def run_small(body, name, here, operands, out_shape, outs=1, limit=VMEM, waits_for=()):
    in_vmem = pl.BlockSpec(memory_space=pltpu.VMEM)

    def whole(*refs):
        body(*refs[: 1 + len(operands)], *refs[1 + len(operands) + len(waits_for) :])

    return pl.pallas_call(
        whole,
        in_specs=[pl.BlockSpec(memory_space=pltpu.SMEM)]
        + [in_vmem] * len(operands)
        + [pl.BlockSpec(memory_space=pltpu.HBM)] * len(waits_for),
        out_specs=[in_vmem] * outs,
        out_shape=[jax.ShapeDtypeStruct(out_shape, jnp.bfloat16)] * outs,
        compiler_params=compiler_params(limit),
        cost_estimate=small_cost(),
        name=name,
    )(here, *operands, *waits_for)


def added(here, *parts, limit=VMEM):
    def body(_, *refs):
        total = refs[0][...].astype(jnp.float32)
        for ref in refs[1:-1]:
            total = total + ref[...].astype(jnp.float32)
        refs[-1][...] = total.astype(jnp.bfloat16)

    return run_small(body, "added", here, parts, parts[0].shape, limit=limit)[0]


def added_pieces(here, one, two, cuts, waits_for):
    steps, _, columns = one.shape
    places = [slice(low, high) for low, high in zip(cuts[:-1], cuts[1:])]

    def body(_, one_ref, two_ref, *refs):
        outs = refs[len(waits_for) :]
        total = one_ref[...].astype(jnp.float32) + two_ref[...].astype(jnp.float32)
        total = total.astype(jnp.bfloat16)
        for place, out in zip(places, outs):
            out[...] = total[:, place]

    in_vmem = pl.BlockSpec(memory_space=pltpu.VMEM)
    return pl.pallas_call(
        body,
        in_specs=[pl.BlockSpec(memory_space=pltpu.SMEM)]
        + [in_vmem] * 2
        + [pl.BlockSpec(memory_space=pltpu.HBM)] * len(waits_for),
        out_specs=[in_vmem] * len(places),
        out_shape=[
            jax.ShapeDtypeStruct((steps, place.stop - place.start, columns), jnp.bfloat16)
            for place in places
        ],
        compiler_params=compiler_params(),
        cost_estimate=small_cost(),
        name="added_pieces",
    )(here, one, two, *waits_for)


def joined(here, ones, twos, waits_for):
    steps, _, columns = ones[0].shape
    count = len(ones)
    ends = [sum(one.shape[1] for one in ones[:at]) for at in range(count + 1)]

    def body(_, *refs):
        for at in range(count):
            total = refs[at][...].astype(jnp.float32) + refs[count + at][...].astype(jnp.float32)
            refs[-1][:, ends[at] : ends[at + 1]] = total.astype(jnp.bfloat16)

    shape = (steps, ends[-1], columns)
    return run_small(body, "joined", here, (*ones, *twos), shape, waits_for=waits_for)[0]


def stacked(here, *parts, waits_for):
    rows = [part.shape[0] for part in parts]

    def body(_, *refs):
        for at, ref in enumerate(refs[:-1]):
            refs[-1][sum(rows[:at]) : sum(rows[: at + 1])] = ref[...]

    shape = (sum(rows), *parts[0].shape[1:])
    return run_small(body, "stacked", here, parts, shape, waits_for=waits_for)[0]


def added_half(here, mine, keep, sends, crossed=None):
    steps, rows, columns = keep.shape
    half, count = steps // 2, len(sends)
    ends = [sum(send.shape[1] for send in sends[:at]) for at in range(count + 1)]

    def body(here_ref, keep_ref, *refs):
        chip = here_ref[2] // 2
        taken = pl.ds((chip if mine else 1 - chip) * half, half)
        for at in range(count):
            place = slice(ends[at], ends[at + 1])
            total = keep_ref[taken, place].astype(jnp.float32) + refs[at][taken].astype(jnp.float32)
            if crossed is not None:
                total = total + refs[count][:, place].astype(jnp.float32)
            refs[-1][:, place] = total.astype(jnp.bfloat16)

    operands = (keep, *sends) if crossed is None else (keep, *sends, crossed)
    return run_small(body, "added_half", here, operands, (half, rows, columns))[0]


def added_halves(here, keep, sends, crossed):
    steps, rows, columns = keep.shape
    half, piece = steps // 2, rows // 2

    def body(here_ref, keep_ref, far_ref, end_ref, crossed_ref, first_ref, second_ref):
        chip = here_ref[2] // 2
        taken = pl.ds(chip * half, half)
        total = keep_ref[taken].astype(jnp.float32) + crossed_ref[...].astype(jnp.float32)
        far = (total[:, :piece] + far_ref[taken].astype(jnp.float32)).astype(jnp.bfloat16)
        end = (total[:, piece:] + end_ref[taken].astype(jnp.float32)).astype(jnp.bfloat16)
        at_home = here_ref[1] // 2 == chip

        @pl.when(at_home)
        def _():
            first_ref[...] = far
            second_ref[...] = end

        @pl.when(jnp.logical_not(at_home))
        def _():
            first_ref[...] = end
            second_ref[...] = far

    shape = (half, piece, columns)
    return run_small(body, "added_halves", here, (keep, *sends, crossed), shape, 2)


def after(value, *others):
    return lax.optimization_barrier((value, *others))[0]


def home_pairs(target, turned):
    pairs = []
    for source in (1, 2):
        side = source // 2
        chip = 1 - side if turned else side
        for at in range(2):
            pairs.append((source * 4 + 2 * chip + at, target(source) * 4 + 2 * side + at))
    return pairs


def sent_home(value, *pairs):
    return lax.ppermute(value, ("samp", "head"), [pair for part in pairs for pair in part])


def across_home(value):
    pairs = [
        (source * 4 + 2 * (1 - source // 2) + at, source * 4 + 2 * (source // 2) + at)
        for source in (1, 2)
        for at in range(2)
    ]
    return lax.ppermute(value, ("samp", "head"), pairs)


def inward_plan(
    prompt_states,
    prompt_lengths,
    prompt_owner,
    kv_weight,
    sampler_prompts,
    step_queries,
    step_kv,
    out_weight,
):
    group, plane, head = (lax.axis_index(name) for name in ("groups", "samp", "head"))
    chip = head // 2
    here = jnp.stack([group, plane, head]).astype(jnp.int32)

    def on_samp(value, pairs):
        return lax.ppermute(value, "samp", pairs)

    def on_head(value, pairs):
        return lax.ppermute(value, "head", pairs)

    def hopped(*values):
        token = here
        for value in values:
            token = on_head(after(token, *value), CORE)
        return token

    def beside(value, *others):
        return on_head(after(value, *others), CORE)

    states = prompt_states[0]
    tokens = states.shape[0]
    cuts = [0, tokens * 7 // 16, tokens]
    sent, kept = project(here, states, kv_weight, (3, 2), cuts)

    half = out_weight.shape[0] // 2
    weight_cuts = [0, half * 2 // 5, half]

    def weight_part(at, *others):
        low, size = weight_cuts[at], weight_cuts[at + 1] - weight_cuts[at]
        return lax.dynamic_slice_in_dim(after(out_weight, *others), group * half + low, size, 0)

    def swapped(part):
        return lax.ppermute(part, "groups", [(0, 1), (1, 0)])

    weight_0 = on_samp(weight_part(0, sent[0]), INWARD)
    leaving_first = added(here, kept[0], on_head(sent[0], CORE), limit=32 * 1024 * 1024)
    leaving_second = added(here, kept[1], after(on_head(sent[1], CORE), leaving_first), limit=32 * 1024 * 1024)
    crossed_first = on_head(leaving_first, ACROSS_X)
    crossed_second = on_head(leaving_second, ACROSS_X)
    sent, kept = project(
        here, after(states, leaving_first, leaving_second), kv_weight, (1, 0), cuts
    )
    sent = [on_head(value, CORE) for value in sent]
    first = added(hopped((crossed_first,)), kept[0], sent[0], crossed_first, limit=32 * 1024 * 1024)
    end_first = on_samp(after(first, weight_0), INWARD)
    far_first = on_samp(first, MIDDLE)
    second = added(here, kept[1], sent[1], crossed_second, limit=32 * 1024 * 1024)
    end_second = on_samp(second, INWARD)
    far_second = on_samp(second, MIDDLE)
    end_page = stacked(
        here, end_first, end_second, waits_for=(beside(leaving_first, far_first, end_first),)
    )
    moved_0 = swapped(weight_0)
    far_end_page = on_samp(after(end_page, far_second), MIDDLE)
    pages = ((first, second), (end_page,), (far_first, far_second), (far_end_page,))
    end_prompts = on_samp(after(sampler_prompts, second), INWARD)
    weight_1 = on_samp(after(weight_part(1, first), end_second, end_prompts), INWARD)
    asked = jnp.concatenate([after(step_queries, first), step_kv], axis=2)
    end_asked = on_samp(after(asked, weight_1), INWARD)
    parts = ((weight_0, moved_0), (weight_1, swapped(weight_1)))
    moved_weights = [
        (low, side, part[side]) for side in range(2) for low, part in zip(weight_cuts, parts)
    ]

    def attended(place, chosen, prompts, queries, news):
        rows = attend(
            chosen, place, prompts, prompt_owner, prompt_lengths, queries, news, pages
        )
        return rows, on_samp(rows, MIDDLE)

    def spread_out(*blocks, waits_for=()):
        keep, sends = spread(here, blocks, out_weight, moved_weights, waits_for)
        return keep, [on_head(send, CORE) for send in sends]

    blocks = sampler_prompts.shape[0]
    own_rows, far_own_rows = attended(
        here, (0, blocks), sampler_prompts, after(step_queries, moved_0), (step_kv, 0)
    )
    end_rows, far_end_rows = attended(
        here,
        (0, blocks),
        end_prompts,
        after(end_asked, own_rows),
        (end_asked, step_queries.shape[2]),
    )
    both_keep, both_arrived = spread_out(far_own_rows, end_rows)
    own_keep, own_arrived = spread_out(after(own_rows, both_keep))
    both_leaving = added_half(here, False, both_keep, both_arrived)
    both_crossed = on_head(both_leaving, ACROSS_X)
    beyond_keep, beyond_arrived = spread_out(
        after(far_end_rows, own_keep, both_leaving),
        waits_for=(beside(own_keep, far_end_rows),),
    )
    beyond_leaving = added_half(here, False, beyond_keep, beyond_arrived)
    beyond_crossed = on_head(beyond_leaving, ACROSS_X)
    own_chip = added_pieces(
        here,
        own_keep,
        after(own_arrived[0], beyond_leaving),
        (0, own_rows.shape[1] * 3 // 4, own_rows.shape[1]),
        waits_for=(beside(own_rows, both_crossed),),
    )
    own_crossed = [
        across_home(after(part, earlier))
        for part, earlier in zip(own_chip, (both_crossed, beyond_crossed))
    ]
    first_sum, second_sum = added_halves(here, both_keep, both_arrived, both_crossed)

    def far(at):
        return 3 - at

    def end(at):
        return at ^ 1

    def beyond(at):
        return (3 - at) ^ 1

    first_home = sent_home(first_sum, home_pairs(far, False), home_pairs(end, True))
    second_home = sent_home(second_sum, home_pairs(far, True), home_pairs(end, False))
    beyond_sum = added_half(
        here, True, beyond_keep, beyond_arrived, beyond_crossed
    )
    beyond_home = [sent_home(beyond_sum, home_pairs(beyond, turned)) for turned in (False, True)]
    own_home = joined(
        here, own_chip, own_crossed, waits_for=(beside(own_keep, own_crossed[0]),)
    )

    is_middle = jnp.logical_or(plane == 1, plane == 2)
    near_side = chip == plane // 2
    straight = jnp.where(is_middle, first_home, jnp.where(near_side, second_home, beyond_home[0]))
    turned = jnp.where(is_middle, second_home, jnp.where(near_side, first_home, beyond_home[1]))
    return jnp.where(
        jnp.logical_and(is_middle, near_side),
        own_home,
        jnp.where(
            chip == 0,
            jnp.concatenate([straight, turned], axis=0),
            jnp.concatenate([turned, straight], axis=0),
        ),
    )


def solution(mesh):
    line, width = mesh.shape["samp"], mesh.shape["head"]
    paired = line == 4 and width == 4 and mesh.shape["groups"] == 2
    on_device = inward_plan if paired else general_plan

    placed = (
        P(("groups", "samp"), None, "head"),
        P("groups"),
        P("groups"),
        P("head", None),
        P(("groups", "samp")),
        P(None, ("groups", "samp"), "head"),
        P(None, ("groups", "samp"), "head"),
        P("head", "samp"),
    )
    return jax.shard_map(
        on_device,
        mesh=mesh,
        in_specs=placed,
        out_specs=P(None, ("groups", "samp"), "head"),
        check_vma=False,
    )
```
